512 devices in a mesh: leaf: 4 (over x), row: 16 (over z, core), col: 8 (over y).
Axes of the slice: x: 4, y: 8, z: 8, core: 2. Of those that a mesh axis runs over, the one named last changes fastest.
Arguments:
- widths: int32 [15], replicated, may hold values from 1024 to 2048, as said below
- bottom_lists: int32 [8, 32], P('leaf'), may hold values from 0 to 47, as said below
- root_inverse: bfloat16 [2048, 2048], P('row')
- second_panels: bfloat16 [4, 2048, 1024], P('leaf', 'row', 'col'), may hold values from -0.09375 to 0.09375
- second_inverse: bfloat16 [4, 1024, 2048], P('leaf', 'col', 'row')
- third_panels: bfloat16 [4, 2, 2048, 2048], P('leaf', None, 'row', 'col'), may hold values from -0.09375 to 0.09375
- third_inverse: bfloat16 [4, 2048, 2048], P('leaf', 'col', 'row')
- bottom_panels: bfloat16 [8, 4096, 2048], P('leaf', 'row', 'col'), may hold values from -0.09375 to 0.09375
- bottom_inverse: bfloat16 [8, 2048, 2048], P('leaf', 'col', 'row')
Outputs:
- second_off: bfloat16 [4, 2048, 1024], P('leaf', 'row', 'col')
- second_diag: bfloat16 [4, 1024, 2048], P('leaf', 'col', 'row')
- third_off: bfloat16 [4, 2, 2048, 2048], P('leaf', None, 'row', 'col')
- third_diag: bfloat16 [4, 2048, 2048], P('leaf', 'col', 'row')
- bottom_off: bfloat16 [8, 3, 2048, 2048], P('leaf', None, 'row', 'col')
- bottom_diag: bfloat16 [8, 2048, 2048], P('leaf', 'col', 'row')
The draws below stay inside these ranges and needn't reach their ends.
Inputs may be any that keep to these rules, and one draw needn't show every extreme that they name: `widths`: some supernode has 2048 columns and some 2048/2. `bottom_lists`: row e lists 32 different blocks of 128 rows of its chain (root, then second-level ancestor, then parent, 16 blocks each) in increasing order; block 0 and all blocks of the parent are always listed.
All inputs are finite; a program needn't handle non-finite values.
Results may differ from the reference program's by a relative error of at most 0.015.
Values may be sent and summed in bfloat16 or wider, within the bound.
A program may use at most 64 MiB of HBM per device.

```python
import jax
import jax.numpy as jnp
from jax import lax

B = 2048
R = 128
NODES = 15
BOTTOM = 8
N_ROW = 16


def symmetric_blocks(key, count):
    base = jax.random.normal(key, (count, B, B), jnp.float32)
    return 0.35 * (base + jnp.swapaxes(base, 1, 2))


def draw_widths(key, part):
    picks = jax.random.randint(jax.random.fold_in(key, 1), (NODES,), B // 2, B + 1)
    order = jax.random.permutation(jax.random.fold_in(key, 2), NODES)
    picks = picks.at[order[0]].set(B).at[order[1]].set(B // 2)
    return picks.astype(jnp.int32)


def draw_bottom_lists(key, part):
    blocks = B // R

    def one_list(sub_key):
        upper_part = jax.random.permutation(sub_key, 2 * blocks - 1)[:blocks - 1] + 1
        chosen = jnp.concatenate([jnp.zeros((1,), jnp.int32), upper_part.astype(jnp.int32), jnp.arange(2 * blocks, 3 * blocks, dtype=jnp.int32)])
        return jnp.sort(chosen)
    return jax.vmap(one_list)(jax.random.split(jax.random.fold_in(key, 3), BOTTOM)).astype(jnp.int32)


def draw_root_inverse(key, part):
    return symmetric_blocks(jax.random.fold_in(key, 4), 1)[0].astype(jnp.bfloat16)


def draw_second_inverse(key, part):
    return symmetric_blocks(jax.random.fold_in(key, 5), 2).reshape(4, B // 2, B).astype(jnp.bfloat16)


def draw_third_inverse(key, part):
    return symmetric_blocks(jax.random.fold_in(key, 6), 4).astype(jnp.bfloat16)


def draw_bottom_inverse(key, part):
    return symmetric_blocks(jax.random.fold_in(key, 7), BOTTOM).astype(jnp.bfloat16)


def steps_of(stream_key, extent, shards, low, high):
    def one(axis_at, blocks):
        draws = jax.random.uniform(jax.random.fold_in(jax.random.fold_in(stream_key, 6), axis_at), (blocks,), jnp.float32, low / len(shards), high / len(shards))
        return jnp.repeat(jnp.exp(draws), extent[axis_at] // blocks).reshape((-1,) + (1,) * (len(extent) - axis_at - 1))

    factor_of = one(*shards[0])
    for cut in shards[1:]:
        factor_of = factor_of * one(*cut)
    return factor_of


def noise(own_key, dims, width, limit, cuts=(), kind=jnp.bfloat16):
    result = jax.random.normal(own_key, dims, jnp.float32) * width
    if len(cuts) > 0:
        result = steps_of(own_key, dims, cuts, -0.22, 0.18) * result
    return jnp.clip(result, min=-limit, max=limit).astype(kind)


def setup_inputs(seed: int = 0) -> dict:
    key_list = jax.random.split(jax.random.key(seed), 10)
    widths = draw_widths(jax.random.fold_in(key_list[9], 71), 0)
    bottom_lists = draw_bottom_lists(jax.random.fold_in(key_list[9], 71), 0)
    root_inverse = draw_root_inverse(jax.random.fold_in(key_list[9], 71), 0)
    second_panels = noise(key_list[3], (4, B, B // 2), (2 * B) ** -0.5, 0.09375, ((0, 4), (1, 16), (2, 8)))
    second_inverse = draw_second_inverse(jax.random.fold_in(key_list[9], 71), 0)
    third_panels = noise(key_list[5], (4, 2, B, B), (2 * B) ** -0.5, 0.09375, ((0, 4), (2, 16), (3, 8)))
    third_inverse = draw_third_inverse(jax.random.fold_in(key_list[9], 71), 0)
    bottom_panels = noise(key_list[7], (BOTTOM, 2 * B, B), (2 * B) ** -0.5, 0.09375, ((0, 4), (1, 16), (2, 8)))
    bottom_inverse = draw_bottom_inverse(jax.random.fold_in(key_list[9], 71), 0)
    return dict(widths=widths, bottom_lists=bottom_lists, root_inverse=root_inverse, second_panels=second_panels, second_inverse=second_inverse, third_panels=third_panels, third_inverse=third_inverse, bottom_panels=bottom_panels, bottom_inverse=bottom_inverse)


def node_mask(widths, node_at):
    return jnp.arange(B) < widths[node_at]


def both_mask(widths, node_at):
    ones_at = node_mask(widths, node_at)
    return ones_at[:, None] & ones_at[None, :]


def partial_sums(lower_rows, upper_rows):
    ancestors = lower_rows.shape[0]
    slab_rows = B // N_ROW
    lower_cut = jnp.transpose(lower_rows.reshape(ancestors, N_ROW, slab_rows, B), (1, 0, 2, 3))
    upper_cut = jnp.transpose(upper_rows.reshape(ancestors, N_ROW, slab_rows, B), (1, 0, 2, 3))

    def add_slab(running, pair_in):
        left_part, right_part = pair_in
        term_slab = jnp.einsum("kin,kim->nm", left_part.astype(jnp.float32), right_part.astype(jnp.float32))
        term_slab = lax.optimization_barrier(term_slab.astype(jnp.bfloat16))
        return running + term_slab.astype(jnp.float32), None

    running, _ = lax.scan(add_slab, jnp.zeros((B, B), jnp.float32), (lower_cut, upper_cut))
    return running


def reference(widths, bottom_lists, root_inverse, second_panels, second_inverse, third_panels, third_inverse, bottom_panels, bottom_inverse):
    root_block = jnp.where(both_mask(widths, 0), root_inverse, 0).astype(jnp.bfloat16)
    off_blocks = []
    diag_blocks = []
    off_halves = []
    diag_halves = []
    for parent in range(2):
        node_at = 1 + parent
        panel_at = jnp.concatenate([second_panels[2 * parent], second_panels[2 * parent + 1]], axis=1)
        panel_at = jnp.where(node_mask(widths, node_at)[None, :], panel_at, 0).astype(jnp.bfloat16)
        off_block = (-jnp.dot(root_block, panel_at, preferred_element_type=jnp.float32)).astype(jnp.bfloat16)
        inverse_at = jnp.concatenate([second_inverse[2 * parent], second_inverse[2 * parent + 1]], axis=0)
        masked_at = jnp.where(both_mask(widths, node_at), inverse_at.astype(jnp.float32), 0.0)
        diag_block = (masked_at - partial_sums(panel_at[None], off_block[None])).astype(jnp.bfloat16)
        off_blocks.append(off_block)
        diag_blocks.append(diag_block)
        off_halves += [off_block[:, : B // 2], off_block[:, B // 2:]]
        diag_halves += [diag_block[: B // 2], diag_block[B // 2:]]
    chains = []
    third_offs = []
    third_diags = []
    for group_at in range(4):
        parent = group_at // 2
        node_at = 3 + group_at
        chain_two = jnp.concatenate([
            jnp.concatenate([root_block, off_blocks[parent]], axis=1),
            jnp.concatenate([off_blocks[parent].T, diag_blocks[parent].T], axis=1)], axis=0)
        panel_at = third_panels[group_at].reshape(2 * B, B)
        panel_at = jnp.where(node_mask(widths, node_at)[None, :], panel_at, 0).astype(jnp.bfloat16)
        off_two = (-jnp.dot(chain_two, panel_at, preferred_element_type=jnp.float32)).astype(jnp.bfloat16)
        masked_at = jnp.where(both_mask(widths, node_at), third_inverse[group_at].astype(jnp.float32), 0.0)
        diag_two = (masked_at - partial_sums(panel_at.reshape(2, B, B), off_two.reshape(2, B, B))).astype(jnp.bfloat16)
        chain_three = jnp.concatenate([
            jnp.concatenate([chain_two, off_two], axis=1),
            jnp.concatenate([off_two.T, diag_two.T], axis=1)], axis=0)
        chains.append(chain_three)
        third_offs.append(off_two.reshape(2, B, B))
        third_diags.append(diag_two)
    spot_list = jnp.arange(2 * B, dtype=jnp.int32)
    bottom_offs = []
    bottom_diags = []
    for bottom in range(BOTTOM):
        node_at = NODES - BOTTOM + bottom
        chain_at = chains[bottom // 2]
        positions = (jnp.repeat(bottom_lists[bottom].astype(jnp.int32), R) * R + spot_list % R).astype(jnp.int32)
        panel_at = jnp.where(node_mask(widths, node_at)[None, :], bottom_panels[bottom], 0).astype(jnp.bfloat16)
        spread = jnp.zeros((3 * B, B), jnp.bfloat16).at[positions].set(panel_at)
        member = jnp.zeros((3 * B,), jnp.bool_).at[positions].set(True)
        product = jnp.dot(chain_at, spread, preferred_element_type=jnp.float32)
        off_three = jnp.where(member[:, None], -product, 0.0).astype(jnp.bfloat16)
        masked_at = jnp.where(both_mask(widths, node_at), bottom_inverse[bottom].astype(jnp.float32), 0.0)
        diag_three = (masked_at - partial_sums(spread.reshape(3, B, B), off_three.reshape(3, B, B))).astype(jnp.bfloat16)
        bottom_offs.append(off_three.reshape(3, B, B))
        bottom_diags.append(diag_three)
    return (jnp.stack(off_halves), jnp.stack(diag_halves), jnp.stack(third_offs), jnp.stack(third_diags),
            jnp.stack(bottom_offs), jnp.stack(bottom_diags))
```

```python
import jax
import jax.numpy as jnp
from jax import lax
from jax.experimental import pallas as pl
from jax.experimental.pallas import tpu as pltpu
from jax.sharding import PartitionSpec as P

NODES = 15
BOTTOM = 8
F32 = jnp.float32
BF16 = jnp.bfloat16
MESH = pl.DeviceIdType.MESH
SEMS = 320
RING = 8


def dot(a, b):
    return jnp.dot(a, b, preferred_element_type=F32)


def wrap(at):
    return lax.rem(at + 2 * RING, RING)


class Links:
    def __init__(self, send, recv):
        self.send, self.recv = send, recv
        self.used = 0
        self.sent = []

    def take(self, count):
        first = self.used
        self.used += count
        assert self.used <= SEMS
        return first

    def copy(self, src, dst, send_at, recv_at, device):
        return pltpu.make_async_remote_copy(
            src_ref=src,
            dst_ref=dst,
            send_sem=self.send.at[send_at],
            recv_sem=self.recv.at[recv_at],
            device_id=device,
            device_id_type=MESH,
        )

    def start(self, src, dst, send_at, recv_at, device):
        made = self.copy(src, dst, send_at, recv_at, device)
        made.start()
        self.sent.append(made)

    def arrived(self, ref, recv_at, device):
        self.copy(ref, ref, recv_at, recv_at, device).wait_recv()

    def drain(self):
        for made in self.sent:
            made.wait_send()


class Gather:
    def __init__(self, links, slot, me, up, down, heard=None):
        self.links, self.slot, self.me = links, slot, me
        self.up, self.down, self.heard = up, down, heard
        self.base = links.take(16)

    def sem(self, way, step, part):
        return self.base + way * 8 + (step - 1) * 2 + part

    def push(self, owner, way, step, part):
        ref = self.slot(owner, part)
        at = self.sem(way, step, part)
        self.links.start(ref, ref, at, at, self.down if way else self.up)

    def begin(self, part):
        self.push(self.me, 0, 1, part)
        self.push(self.me, 1, 1, part)
        if self.heard is not None:
            self.heard(self.me, part)

    def relay(self, step, part):
        if step == 4:
            ways = (part,)
        else:
            ways = (0, 1)
        for way in ways:
            owner = wrap(self.me + step) if way else wrap(self.me - step)
            self.links.arrived(self.slot(owner, part), self.sem(way, step, part), self.up)
            if step < 3 or (step == 3 and way == part):
                self.push(owner, way, step + 1, part)
            if self.heard is not None:
                self.heard(owner, part)

    def both(self, step):
        self.relay(step, 0)
        self.relay(step, 1)


def kernel(
    widths,
    lists,
    root,
    p1,
    e1,
    p2,
    e2,
    p3,
    e3,
    o1,
    d1,
    o2,
    d2,
    o3,
    d3,
    l1g,
    e1x,
    l2g,
    wg,
    ga,
    gb,
    gc,
    gd,
    ot1,
    ot2,
    acc,
    acc3,
    o3f,
    wt,
    term,
    sib,
    stage,
    landed,
    send,
    recv,
):
    g = lax.axis_index("leaf")
    r = lax.axis_index("row")
    c = lax.axis_index("col")
    z = lax.div(r, 2)
    k = lax.rem(r, 2)
    h = lax.rem(g, 2)
    links = Links(send, recv)
    z_up, z_down = {"row": lax.rem(r + 2, 16)}, {"row": lax.rem(r + 14, 16)}
    y_up, y_down = {"col": wrap(c + 1)}, {"col": wrap(c - 1)}
    other_core = {"row": r + 1 - 2 * k}
    other_leaf = {"leaf": g + 1 - 2 * h}

    barrier = pltpu.get_barrier_semaphore()
    for device in (z_up, z_down, y_up, y_down, other_core, other_leaf):
        pl.semaphore_signal(barrier, inc=1, device_id=device, device_id_type=MESH)
    for source in range(16):
        for column in (lax.rem(r, 8), lax.div(r, 2)):
            pl.semaphore_signal(
                barrier, inc=1, device_id={"row": source, "col": column}, device_id_type=MESH
            )

    w0, w1, w2 = widths[0], widths[1 + lax.div(g, 2)], widths[3 + g]
    lane128 = lax.broadcasted_iota(jnp.int32, (128, 128), 1)
    row128 = lax.broadcasted_iota(jnp.int32, (128, 128), 0)
    lane256 = lax.broadcasted_iota(jnp.int32, (128, 256), 1)
    row_at = r * 128

    l1g[h, r] = jnp.where(h * 1024 + c * 128 + lane128 < w1, p1[0].astype(F32), 0.0).astype(BF16)
    pl.semaphore_wait(barrier, 38)

    x_at = links.take(2)
    links.start(l1g.at[h, r], l1g.at[h, r], x_at, x_at, other_leaf)
    links.start(e1.at[0], e1x.at[h], x_at + 1, x_at + 1, other_leaf)

    def z_gather(slot):
        base = links.take(16)

        def heard(owner, part):
            ref = slot(2 * owner + k, part)
            at = base + owner * 2 + part
            links.start(ref, ref, at, at, other_core)

        def finish():
            for owner in range(RING):
                for part in range(2):
                    links.arrived(slot(2 * owner + 1 - k, part), base + owner * 2 + part, other_core)

        ring = Gather(links, lambda owner, part: slot(2 * owner + k, part), z, z_up, z_down, heard)
        return ring, finish

    ring_l1, finish_l1 = z_gather(lambda who, part: l1g.at[1 - h if part else h, who])
    ring_l2, finish_l2 = z_gather(lambda who, part: l2g.at[part * 16 + who])
    ring_w, finish_w = z_gather(
        lambda who, part: wg.at[part, pl.ds(pl.multiple_of(2 * who, 2), 2)]
    )

    ring_l1.begin(0)
    links.arrived(l1g.at[1 - h, r], x_at, other_leaf)
    ring_l1.begin(1)

    def mask_root(b, carry):
        cols = b * 128 + lane128
        keep = (row_at + row128 < w0) & (cols < w0)
        block = root[:, pl.ds(pl.multiple_of(b * 128, 128), 128)].astype(F32)
        ga[b, 0:128] = jnp.where(keep, block, 0.0).astype(BF16)
        return carry

    lax.fori_loop(0, 16, mask_root, 0)
    own256 = c * 256 + lane256
    for part in range(2):
        l2g[part * 16 + r] = jnp.where(own256 < w2, p2[0, part].astype(F32), 0.0).astype(BF16)
    ring_l1.both(1)
    ring_l1.both(2)
    ring_l2.begin(0)
    ring_l2.begin(1)
    ring_l1.both(3)
    ring_l1.both(4)
    for e in range(2):
        w3 = widths[NODES - BOTTOM + 2 * g + e]
        for u in range(2):
            wg[e, 2 * r + u] = jnp.where(
                own256 < w3, p3[e, u * 128 : u * 128 + 128].astype(F32), 0.0
            ).astype(BF16)
    e1x[h] = e1[0]
    finish_l1()

    def product(target, lhs, rhs, count, fresh=True):
        if fresh:
            target[...] = jnp.zeros(target.shape, F32)

        def body(q, carry):
            target[...] += dot(lhs(q), rhs(q))
            return carry

        lax.fori_loop(0, count, body, 0)

    def wide(ref, blocks, rows=None):
        if rows is None:
            return jnp.concatenate([ref[b] for b in blocks], axis=1)
        return jnp.concatenate([ref[b, rows] for b in blocks], axis=1)

    def panel_one(q):
        return jnp.concatenate(
            [l1g[half, pl.ds(4 * q, 4)].reshape(512, 128) for half in range(2)], axis=1
        )

    top = slice(0, 128)
    mid = slice(128, 256)
    four = lambda q: [4 * q + u for u in range(4)]
    product(acc.at[top], lambda q: wide(ga, four(q), top), panel_one, 4)
    off = -acc[top]
    for half in range(2):
        block = off[:, half * 128 : half * 128 + 128]
        ga[16 + 8 * half + c, top] = block.astype(BF16)
        ot1[half] = block.T.astype(BF16)
    o1[0] = ga[16 + 8 * h + c, top]

    def sixteen(start, at):
        return pl.ds(pl.multiple_of(start + 16 * at, 16), 16)

    def turn(source, slot, dest_row):
        sends = links.take(16)
        first = links.take(16)
        for t in range(2):
            row_to = dest_row(t)
            for apart in range(RING):
                y = wrap(c + apart)
                src = source(t, y)
                dst = slot(r, y)
                at = sends + t * RING + apart
                made = links.copy(src, dst, at, first + r, {"row": row_to, "col": y})
                if apart == 0:
                    local = pltpu.make_async_copy(src, dst, links.recv.at[first + r])
                    pl.when(row_to == r)(local.start)
                    pl.when(row_to != r)(made.start)

                    def wait_made(made=made, row_to=row_to):
                        pl.when(row_to != r)(made.wait_send)

                    waits.append(wait_made)
                else:
                    made.start()
                    links.sent.append(made)

        def finish():
            for source_row in range(16):
                links.arrived(slot(source_row, c), first + source_row, y_up)

        return finish

    waits = []
    finish_t1 = turn(
        lambda t, y: ot1.at[t, sixteen(0, y)],
        lambda who, y: ga.at[who, sixteen(128, y)],
        lambda t: 8 * t + c,
    )
    y_gather = lambda slot: Gather(links, slot, c, y_up, y_down)
    ring_o1 = y_gather(lambda who, part: ga.at[16 + 8 * part + who, top])
    ring_t1 = y_gather(lambda who, part: ga.at[pl.ds(8 * part, 8), sixteen(128, who)])
    ring_d1 = y_gather(lambda who, part: ga.at[16 + 8 * part + who, mid])
    ring_o2 = y_gather(lambda who, part: gb.at[who, pl.ds(128 * part, 128)])
    ring_t2 = y_gather(lambda who, part: gc.at[pl.ds(16 * part, 16), sixteen(0, who)])
    ring_d2 = y_gather(lambda who, part: gd.at[who, pl.ds(64 * part, 64)])
    ring_o3 = y_gather(lambda who, part: o3f.at[part, who])

    finish_t1()
    ring_t1.begin(0)
    ring_t1.begin(1)
    ring_o1.begin(0)
    ring_o1.begin(1)
    ring_l2.both(1)
    ring_t1.both(1)
    ring_t1.both(2)
    ring_l2.both(2)
    ring_t1.both(3)
    ring_o1.both(1)
    ring_t1.both(4)

    links.arrived(e1x.at[1 - h], x_at + 1, other_leaf)
    product(acc.at[top], lambda q: wide(ga, four(q), mid), panel_one, 4)
    for half in range(2):
        keep = (half * 1024 + c * 128 + lane128 < w1) & (row_at + row128 < w1)
        given = jnp.where(keep, e1x[half].astype(F32).T, 0.0)
        turned = given - acc[top, half * 128 : half * 128 + 128]
        ga[16 + 8 * half + c, mid] = turned.astype(BF16)
    ring_d1.begin(0)
    ring_d1.begin(1)
    d1[0] = ga[16 + 8 * h + c, mid].astype(F32).T.astype(BF16)
    ring_l2.both(3)
    ring_o1.both(2)
    ring_d1.both(1)
    ring_l2.both(4)
    ring_w.begin(0)
    ring_w.begin(1)
    ring_o1.both(3)
    ring_d1.both(2)
    ring_o1.both(4)
    ring_d1.both(3)
    finish_l2()
    ring_d1.both(4)

    panel_two = lambda q: l2g[pl.ds(4 * q, 4)].reshape(512, 256)
    product(acc, lambda q: wide(ga, four(q)), panel_two, 8)
    for a in range(2):
        rows = slice(128 * a, 128 * a + 128)
        off = -acc[rows]
        gb[c, rows] = off.astype(BF16)
        for t in range(2):
            ot2[t, a] = off[:, t * 128 : t * 128 + 128].T.astype(BF16)
    finish_t2 = turn(
        lambda t, y: ot2.at[t, :, sixteen(0, y)],
        lambda who, y: gc.at[pl.ds(pl.multiple_of(2 * who, 2), 2), sixteen(0, y)],
        lambda t: 2 * c + t,
    )
    for a in range(2):
        o2[0, a] = gb[c, 128 * a : 128 * a + 128]
    ring_w.both(1)
    finish_t2()
    ring_t2.begin(0)
    ring_t2.begin(1)
    ring_o2.begin(0)
    ring_o2.begin(1)
    ring_t2.both(1)
    ring_t2.both(2)
    ring_w.both(2)
    ring_t2.both(3)
    ring_o2.both(1)
    ring_t2.both(4)

    def panel_turned(q):
        return jnp.concatenate(
            [l2g[2 * q], l2g[16 + 2 * q], l2g[2 * q + 1], l2g[17 + 2 * q]], axis=0
        )

    product(acc.at[top], lambda q: wide(gc, four(q)), panel_turned, 8)
    for half in range(2):
        cols = slice(half * 128, half * 128 + 128)
        keep = (c * 256 + half * 128 + lane128 < w2) & (row_at + row128 < w2)
        given = jnp.where(keep, e2[0, cols].astype(F32).T, 0.0)
        turned = (given - acc[top, cols]).astype(BF16)
        gd[c, :, cols] = turned
        d2[0, cols] = turned.astype(F32).T.astype(BF16)
    ring_d2.begin(0)
    ring_d2.begin(1)
    ring_w.both(3)
    ring_o2.both(2)
    ring_d2.both(1)
    ring_w.both(4)
    ring_o2.both(3)
    ring_d2.both(2)
    ring_o2.both(4)
    ring_d2.both(3)
    finish_w()

    low = slice(256, 384)
    for e in range(2):
        panel = lambda q, e=e: wg[e, pl.ds(4 * q, 4)].reshape(512, 256)
        listed = lambda q, e=e: [lists[e, 4 * q + u] for u in range(4)]
        turned = lambda q, e=e: [
            2 * lax.bitwise_and(b, 15) + lax.shift_right_logical(b, 4) for b in listed(q)
        ]
        product(acc3.at[e, 0:256], lambda q: wide(ga, listed(q)), panel, 4)
        product(acc3.at[e, low], lambda q: wide(gc, turned(q)), panel, 4)
    places = []
    for e in range(2):
        row = []
        for a in range(2):
            found, where = jnp.int32(0), jnp.int32(0)
            for i in range(16):
                hit = lists[e, i] == 16 * a + r
                found, where = jnp.where(hit, 1, found), jnp.where(hit, i, where)
            row.append((found, where))
        row.append((jnp.int32(1), 16 + r))
        places.append(row)
        for a in range(3):
            wt[e, :, 128 * a : 128 * a + 128] = wg[e, row[a][1]].astype(F32).T.astype(BF16)
    ring_d2.both(4)
    for e in range(2):
        parent = lambda q, e=e: wg[e, pl.ds(16 + 4 * q, 4)].reshape(512, 256)
        pair = lambda q: [2 * q, 2 * q + 1]
        product(acc3.at[e, 0:256], lambda q: wide(gb, pair(q)), parent, 4, False)
        product(acc3.at[e, low], lambda q: wide(gd, pair(q)), parent, 4, False)
        for a in range(3):
            rows = slice(128 * a, 128 * a + 128)
            keep = places[e][a][0] > 0
            off = jnp.where(keep, -acc3[e, rows], 0.0).astype(BF16)
            o3f[e, c, rows] = off
            o3[e, a] = off
        ring_o3.begin(e)

    base_sib = links.take(16)

    def update(e, who):
        both = dot(wt[e], o3f[e, who])
        for t in range(2):
            term[t, e, who] = both[:, t * 128 : t * 128 + 128].astype(BF16)
        at = base_sib + e * RING + who
        links.start(term.at[1 - k, e, who], sib.at[e, who], at, at, other_core)

    for e in range(2):
        update(e, c)
    for step in range(1, 5):
        for e in range(2):
            ring_o3.relay(step, e)
            update(e, wrap(c - step))
            if step < 4:
                update(e, wrap(c + step))
    for e in range(2):
        for who in range(RING):
            links.arrived(sib.at[e, who], base_sib + e * RING + who, other_core)

    def mine(e, who):
        return term[k, e, who].astype(F32) + sib[e, who].astype(F32)

    base_sum = links.take(16)
    arm = lambda e, way: 4 if way == e else 3
    slot_sum = lambda e, way, step: (e * 2 + way) * 4 + step - 1
    for step in range(1, 5):
        for e in range(2):
            for way in range(2):
                if step > arm(e, way):
                    continue
                apart = arm(e, way) + 1 - step
                value = mine(e, wrap(z - apart) if way else wrap(z + apart))
                at = slot_sum(e, way, step)
                if step > 1:
                    links.arrived(landed.at[at - 1], base_sum + at - 1, z_up)
                    value = value + landed[at - 1].astype(F32)
                stage[at] = value.astype(BF16)
                links.start(
                    stage.at[at],
                    landed.at[at],
                    base_sum + at,
                    base_sum + at,
                    z_down if way else z_up,
                )
    rows256 = lax.broadcasted_iota(jnp.int32, (256, 128), 0)
    cols256 = lax.broadcasted_iota(jnp.int32, (256, 128), 1)
    for e in range(2):
        w3 = widths[NODES - BOTTOM + 2 * g + e]
        total = mine(e, z)
        for way in range(2):
            at = slot_sum(e, way, arm(e, way))
            links.arrived(landed.at[at], base_sum + at, z_up)
            total = total + landed[at].astype(F32)
        keep = (c * 256 + rows256 < w3) & (row_at + cols256 < w3)
        d3[e] = (jnp.where(keep, e3[e].astype(F32), 0.0) - total).astype(BF16)
    links.drain()
    for wait in waits:
        wait()


def local(widths, lists, root, p1, e1, p2, e2, p3, e3):
    vmem = pl.BlockSpec(memory_space=pltpu.VMEM)
    smem = pl.BlockSpec(memory_space=pltpu.SMEM)
    shapes = [(1, 128, 128), (1, 128, 128), (1, 2, 128, 256), (1, 256, 128), (2, 3, 128, 256), (2, 256, 128)]
    scratch = [
        ((2, 16, 128, 128), BF16),
        ((2, 128, 128), BF16),
        ((32, 128, 256), BF16),
        ((2, 32, 128, 256), BF16),
        ((32, 256, 128), BF16),
        ((8, 256, 256), BF16),
        ((32, 128, 128), BF16),
        ((8, 128, 256), BF16),
        ((2, 128, 128), BF16),
        ((2, 2, 128, 128), BF16),
        ((256, 256), F32),
        ((2, 384, 256), F32),
        ((2, 8, 384, 256), BF16),
        ((2, 256, 384), BF16),
        ((2, 2, 8, 256, 128), BF16),
        ((2, 8, 256, 128), BF16),
        ((16, 256, 128), BF16),
        ((16, 256, 128), BF16),
    ]
    return pl.pallas_call(
        kernel,
        out_shape=[jax.ShapeDtypeStruct(shape, BF16) for shape in shapes],
        in_specs=[smem, smem] + [vmem] * 7,
        out_specs=[vmem] * 6,
        scratch_shapes=[pltpu.VMEM(*one) for one in scratch]
        + [pltpu.SemaphoreType.DMA((SEMS,)), pltpu.SemaphoreType.DMA((SEMS,))],
        compiler_params=pltpu.CompilerParams(
            collective_id=0, has_side_effects=True, vmem_limit_bytes=48 * 1024 * 1024
        ),
    )(widths, lists, root, p1, e1, p2, e2, p3, e3)


def solution(mesh):
    in_specs = (
        P(),
        P("leaf", None),
        P("row", None),
        P("leaf", "row", "col"),
        P("leaf", "col", "row"),
        P("leaf", None, "row", "col"),
        P("leaf", "col", "row"),
        P("leaf", "row", "col"),
        P("leaf", "col", "row"),
    )
    out_specs = (
        P("leaf", "row", "col"),
        P("leaf", "col", "row"),
        P("leaf", None, "row", "col"),
        P("leaf", "col", "row"),
        P("leaf", None, "row", "col"),
        P("leaf", "col", "row"),
    )

    def whole(*args):
        return tuple(
            jax.shard_map(
                lambda *own: tuple(local(*own)),
                mesh=mesh,
                in_specs=in_specs,
                out_specs=out_specs,
                check_vma=False,
            )(*args)
        )

    return whole
```

```python
import jax
import jax.numpy as jnp
from jax import lax
from jax.experimental import pallas as pl
from jax.experimental.pallas import tpu as pltpu
from jax.sharding import PartitionSpec as P

NODES = 15
BOTTOM = 8
F32 = jnp.float32
BF16 = jnp.bfloat16
MESH = pl.DeviceIdType.MESH
SEMS = 384
VMEM = 63 * 1024 * 1024
RING = 8


def dot(a, b):
    return jnp.dot(a, b, preferred_element_type=F32)


def wrap(at):
    return lax.rem(at + 2 * RING, RING)


class Links:
    def __init__(self, send, recv):
        self.send, self.recv = send, recv
        self.used = 0
        self.sent = []

    def take(self, count):
        first = self.used
        self.used += count
        assert self.used <= SEMS
        return first

    def copy(self, src, dst, send_at, recv_at, device):
        return pltpu.make_async_remote_copy(
            src_ref=src,
            dst_ref=dst,
            send_sem=self.send.at[send_at],
            recv_sem=self.recv.at[recv_at],
            device_id=device,
            device_id_type=MESH,
        )

    def start(self, src, dst, send_at, recv_at, device):
        made = self.copy(src, dst, send_at, recv_at, device)
        made.start()
        self.sent.append(made)

    def arrived(self, ref, recv_at, device):
        self.copy(ref, ref, recv_at, recv_at, device).wait_recv()

    def drain(self):
        for made in self.sent:
            made.wait_send()


class Gather:
    def __init__(self, links, slot, me, up, down, heard=None, split=False):
        self.links, self.slot, self.me = links, slot, me
        self.up, self.down, self.heard, self.split = up, down, heard, split
        self.base = links.take(16)

    def sem(self, way, step, part):
        return self.base + way * 8 + (step - 1) * 2 + (part or 0)

    def push(self, owner, way, step, part):
        ref = self.slot(owner, part)
        at = self.sem(way, step, part)
        self.links.start(ref, ref, at, at, self.down if way else self.up)

    def begin(self, part=None):
        self.push(self.me, 0, 1, part)
        self.push(self.me, 1, 1, part)
        if self.heard is not None:
            self.heard(self.me, part)

    def relay(self, step, part=None):
        if step == 4:
            for way in (0, 1) if part is None else (part,):
                owner = wrap(self.me + 4)
                self.links.arrived(self.slot(owner, way), self.sem(way, 4, way), self.up)
            if self.heard is not None:
                self.heard(wrap(self.me + 4), part)
            return
        for way in (0, 1):
            owner = wrap(self.me + step) if way else wrap(self.me - step)
            self.links.arrived(self.slot(owner, part), self.sem(way, step, part), self.up)
            if step < 3:
                self.push(owner, way, step + 1, part)
            elif part is None or way == part:
                self.push(owner, way, 4, way)
            if self.heard is not None:
                self.heard(owner, part)

    def both(self, step):
        if self.split:
            self.relay(step, 0)
            self.relay(step, 1)
        else:
            self.relay(step)


def kernel(
    widths,
    lists,
    root_in,
    p1_in,
    e1_in,
    p2_in,
    e2_in,
    p3_in,
    e3_in,
    o1,
    d1,
    o2,
    d2,
    o3,
    d3,
    l1g,
    e1x,
    l2g,
    wg,
    ga,
    gb,
    gc,
    gd,
    ot1,
    ot2,
    acc,
    acc3,
    o3f,
    wt,
    term,
    sib,
    stage,
    landed,
    o3z,
    wtt,
    ot3,
    moved,
    arrived_at,
    root,
    p1,
    e1,
    p2,
    e2,
    p3,
    e3,
    send,
    recv,
    load_sem,
):
    g = lax.axis_index("leaf")
    r = lax.axis_index("row")
    c = lax.axis_index("col")
    z = lax.div(r, 2)
    k = lax.rem(r, 2)
    h = lax.rem(g, 2)
    links = Links(send, recv)
    waits = []
    z_up, z_down = {"row": lax.rem(r + 2, 16)}, {"row": lax.rem(r + 14, 16)}
    y_up, y_down = {"col": wrap(c + 1)}, {"col": wrap(c - 1)}
    other_core = {"row": r + 1 - 2 * k}
    other_leaf = {"leaf": g + 1 - 2 * h}

    barrier = pltpu.get_barrier_semaphore()
    greeted = [z_up, z_down, other_core, other_leaf] + [{"col": wrap(c + d)} for d in range(1, RING)]
    for device in greeted:
        pl.semaphore_signal(barrier, inc=1, device_id=device, device_id_type=MESH)
    loads = {}
    pairs = dict(
        p1=(p1_in, p1), root=(root_in, root), e1=(e1_in, e1), p2=(p2_in, p2),
        p3=(p3_in, p3), e2=(e2_in, e2), e3=(e3_in, e3),
    )
    for at, name in enumerate(pairs):
        loads[name] = pltpu.make_async_copy(*pairs[name], load_sem.at[at])
        loads[name].start()

    w0, w1, w2 = widths[0], widths[1 + lax.div(g, 2)], widths[3 + g]
    lane128 = lax.broadcasted_iota(jnp.int32, (128, 128), 1)
    row128 = lax.broadcasted_iota(jnp.int32, (128, 128), 0)
    lane256 = lax.broadcasted_iota(jnp.int32, (128, 256), 1)
    row_at = r * 128

    loads['p1'].wait()
    l1g[h, r] = jnp.where(h * 1024 + c * 128 + lane128 < w1, p1[0].astype(F32), 0.0).astype(BF16)
    loads['e1'].wait()
    pl.semaphore_wait(barrier, len(greeted))

    x_at = links.take(2)
    links.start(l1g.at[h, r], l1g.at[h, r], x_at, x_at, other_leaf)
    links.start(e1.at[0], e1x.at[h], x_at + 1, x_at + 1, other_leaf)

    def z_gather(slot, split=False):
        base = links.take(16)

        def heard(owner, part):
            ref = slot(2 * owner + k, part)
            at = base + owner * 2 + (part or 0)
            links.start(ref, ref, at, at, other_core)

        def finish():
            for owner in range(RING):
                for part in (0, 1) if split else (None,):
                    at = base + owner * 2 + (part or 0)
                    links.arrived(slot(2 * owner + 1 - k, part), at, other_core)

        mine = lambda owner, part: slot(2 * owner + k, part)
        return Gather(links, mine, z, z_up, z_down, heard, split), finish

    def halves(part, size):
        return pl.ds(0, size) if part is None else pl.ds(part * (size // 2), size // 2)

    def run(start, count):
        return pl.ds(pl.multiple_of(start, count), count)

    ring_l1, finish_l1 = z_gather(lambda who, part: l1g.at[1 - h if part else h, who], True)
    ring_l2, finish_l2 = z_gather(lambda who, part: l2g.at[run(2 * who, 2), halves(part, 128)])
    ring_w, finish_w = z_gather(lambda who, part: wg.at[halves(part, 2), run(2 * who, 2)])
    ring_oz, finish_oz = z_gather(lambda who, part: o3z.at[pl.ds(3 * who, 3), halves(part, 128)])

    ring_l1.begin(0)
    links.arrived(l1g.at[1 - h, r], x_at, other_leaf)
    ring_l1.begin(1)

    def mask_root(b, carry):
        cols = b * 128 + lane128
        keep = (row_at + row128 < w0) & (cols < w0)
        block = root[:, pl.ds(pl.multiple_of(b * 128, 128), 128)].astype(F32)
        ga[b, 0:128] = jnp.where(keep, block, 0.0).astype(BF16)
        return carry

    loads['root'].wait()
    lax.fori_loop(0, 16, mask_root, 0)
    own256 = c * 256 + lane256
    loads['p2'].wait()
    for part in range(2):
        l2g[2 * r + part] = jnp.where(own256 < w2, p2[0, part].astype(F32), 0.0).astype(BF16)
    ring_l1.both(1)
    ring_l1.both(2)
    ring_l2.begin()
    ring_l1.both(3)
    ring_l1.both(4)
    loads['p3'].wait()
    for e in range(2):
        w3 = widths[NODES - BOTTOM + 2 * g + e]
        for u in range(2):
            wg[e, 2 * r + u] = jnp.where(
                own256 < w3, p3[e, u * 128 : u * 128 + 128].astype(F32), 0.0
            ).astype(BF16)
    e1x[h] = e1[0]
    for u in range(2):
        for t in range(2):
            ot3[t, u] = wg[0, 2 * r + u, :, t * 128 : t * 128 + 128].astype(F32).T.astype(BF16)
    finish_l1()

    def product(target, lhs, rhs, count, fresh=True):
        if fresh:
            target[...] = jnp.zeros(target.shape, F32)

        def body(q, carry):
            target[...] += dot(lhs(q), rhs(q))
            return carry

        lax.fori_loop(0, count, body, 0)

    def wide(ref, blocks, rows=None):
        if rows is None:
            return jnp.concatenate([ref[b] for b in blocks], axis=1)
        return jnp.concatenate([ref[b, rows] for b in blocks], axis=1)

    def panel_one(q):
        return jnp.concatenate(
            [l1g[half, pl.ds(4 * q, 4)].reshape(512, 128) for half in range(2)], axis=1
        )

    top = slice(0, 128)
    mid = slice(128, 256)
    four = lambda q: [4 * q + u for u in range(4)]
    product(acc.at[top], lambda q: wide(ga, four(q), top), panel_one, 4)
    off = -acc[top]
    for half in range(2):
        block = off[:, half * 128 : half * 128 + 128]
        ga[16 + 2 * c + half, top] = block.astype(BF16)
        ot1[half] = block.T.astype(BF16)
    o1[0] = ga[16 + 2 * c + h, top]

    def sixteen(start, at):
        return pl.ds(pl.multiple_of(start + 16 * at, 16), 16)

    def turn(source, slot, dest_row):
        sends = links.take(16)
        first = links.take(16)
        for t in range(2):
            row_to = dest_row(t)
            for apart in range(RING):
                y = wrap(c + apart)
                src = source(t, y)
                dst = slot(r, y)
                at = sends + t * RING + apart
                made = links.copy(src, dst, at, first + r, {"row": row_to, "col": y})
                if apart == 0:
                    local = pltpu.make_async_copy(src, dst, links.recv.at[first + r])
                    pl.when(row_to == r)(local.start)
                    pl.when(row_to != r)(made.start)

                    def wait_made(made=made, row_to=row_to):
                        pl.when(row_to != r)(made.wait_send)

                    waits.append(wait_made)
                else:
                    made.start()
                    links.sent.append(made)

        def finish():
            for source_row in range(16):
                links.arrived(slot(source_row, c), first + source_row, y_up)

        return finish

    finish_t1 = turn(
        lambda t, y: ot1.at[t, sixteen(0, y)],
        lambda who, y: ga.at[who, sixteen(128, y)],
        lambda t: 8 * t + c,
    )
    y_gather = lambda slot: Gather(links, slot, c, y_up, y_down)
    ring_o1 = y_gather(
        lambda who, part: ga.at[run(16 + 2 * who, 2) if part is None else 16 + 2 * who + part, top]
    )
    ring_t1 = y_gather(lambda who, part: ga.at[halves(part, 16), sixteen(128, who)])
    ring_d1 = y_gather(
        lambda who, part: ga.at[run(16 + 2 * who, 2) if part is None else 16 + 2 * who + part, mid]
    )
    ring_o2 = y_gather(lambda who, part: gb.at[who, halves(part, 256)])
    ring_t2 = y_gather(lambda who, part: gc.at[halves(part, 32), sixteen(0, who)])
    ring_wt = y_gather(lambda who, part: wtt.at[halves(part, 32), sixteen(0, who)])
    ring_d2 = y_gather(lambda who, part: gd.at[who, halves(part, 128)])
    ring_o3 = y_gather(lambda who, part: o3f.at[who, pl.ds(192 * part, 192) if part is not None else pl.ds(0, 384)])

    finish_t3 = turn(
        lambda t, y: ot3.at[t, :, sixteen(0, y)],
        lambda who, y: wtt.at[run(2 * who, 2), sixteen(0, y)],
        lambda t: 2 * c + t,
    )
    finish_t1()
    ring_t1.begin()
    ring_o1.begin()
    ring_l2.both(1)
    ring_t1.both(1)
    ring_l2.both(2)
    ring_t1.both(2)
    ring_t1.both(3)
    ring_o1.both(1)
    finish_t3()
    ring_wt.begin()
    ring_t1.both(4)

    links.arrived(e1x.at[1 - h], x_at + 1, other_leaf)
    product(acc.at[top], lambda q: wide(ga, four(q), mid), panel_one, 4)
    for half in range(2):
        keep = (half * 1024 + c * 128 + lane128 < w1) & (row_at + row128 < w1)
        given = jnp.where(keep, e1x[half].astype(F32).T, 0.0)
        turned = given - acc[top, half * 128 : half * 128 + 128]
        ga[16 + 2 * c + half, mid] = turned.astype(BF16)
    ring_d1.begin()
    ring_l2.both(3)
    ring_o1.both(2)
    ring_d1.both(1)
    d1[0] = ga[16 + 2 * c + h, mid].astype(F32).T.astype(BF16)
    ring_l2.both(4)
    ring_w.begin()
    ring_o1.both(3)
    ring_d1.both(2)
    ring_wt.both(1)
    ring_d1.both(3)
    ring_o1.both(4)
    finish_l2()
    ring_w.both(1)
    ring_d1.both(4)

    panel_two = lambda q: l2g[pl.ds(4 * q, 4)].reshape(512, 256)
    second = lambda b: 16 + 2 * lax.bitwise_and(b, 7) + lax.shift_right_logical(b, 3)
    crossed = lambda q: [2 * q, second(2 * q), 2 * q + 1, second(2 * q + 1)]
    product(acc, lambda q: wide(ga, crossed(q)), panel_two, 8)
    for a in range(2):
        rows = slice(128 * a, 128 * a + 128)
        off = -acc[rows]
        gb[c, rows] = off.astype(BF16)
        for t in range(2):
            ot2[t, a] = off[:, t * 128 : t * 128 + 128].T.astype(BF16)
    finish_t2 = turn(
        lambda t, y: ot2.at[t, :, sixteen(0, y)],
        lambda who, y: gc.at[pl.ds(pl.multiple_of(2 * who, 2), 2), sixteen(0, y)],
        lambda t: 2 * c + t,
    )
    for a in range(2):
        o2[0, a] = gb[c, 128 * a : 128 * a + 128]
    ring_wt.both(2)
    finish_t2()
    ring_t2.begin()
    ring_o2.begin()
    ring_w.both(2)
    ring_t2.both(1)
    ring_t2.both(2)
    ring_w.both(3)
    ring_t2.both(3)
    ring_o2.both(1)
    ring_t2.both(4)

    loads['e2'].wait()
    product(acc.at[top], lambda q: wide(gc, four(q)), panel_two, 8)
    for half in range(2):
        cols = slice(half * 128, half * 128 + 128)
        keep = (c * 256 + half * 128 + lane128 < w2) & (row_at + row128 < w2)
        given = jnp.where(keep, e2[0, cols].astype(F32).T, 0.0)
        turned = (given - acc[top, cols]).astype(BF16)
        gd[c, :, cols] = turned
        d2[0, cols] = turned.astype(F32).T.astype(BF16)
    ring_d2.begin()
    ring_w.both(4)
    ring_o2.both(2)
    ring_d2.both(1)
    ring_o2.both(3)
    ring_d2.both(2)
    ring_d2.both(3)
    ring_o2.both(4)
    ring_wt.both(3)
    finish_w()

    low = slice(256, 384)
    def placed(b):
        return jnp.where(b < 16, b, second(lax.bitwise_and(b, 15)))

    def paired(b):
        return 2 * lax.bitwise_and(b, 15) + lax.shift_right_logical(b, 4)

    for e in range(2):
        panel = lambda q, e=e: wg[e, pl.ds(4 * q, 4)].reshape(512, 256)
        listed = lambda q, e=e: [lists[e, 4 * q + u] for u in range(4)]
        product(acc3.at[e, 0:256], lambda q: wide(ga, [placed(b) for b in listed(q)]), panel, 4)
        product(acc3.at[e, low], lambda q: wide(gc, [paired(b) for b in listed(q)]), panel, 4)
    places = []
    for e in range(2):
        row = []
        for a in range(2):
            found, where = jnp.int32(0), jnp.int32(0)
            for i in range(16):
                hit = lists[e, i] == 16 * a + r
                found, where = jnp.where(hit, 1, found), jnp.where(hit, i, where)
            row.append((found, where))
        row.append((jnp.int32(1), 16 + r))
        places.append(row)
        for a in range(3):
            if e == 1:
                wt[:, 128 * a : 128 * a + 128] = wg[e, row[a][1]].astype(F32).T.astype(BF16)
    ring_d2.both(4)
    for e in range(2):
        parent = lambda q, e=e: wg[e, pl.ds(16 + 4 * q, 4)].reshape(512, 256)
        pair = lambda q: [2 * q, 2 * q + 1]
        product(acc3.at[e, 0:256], lambda q: wide(gb, pair(q)), parent, 4, False)
        product(acc3.at[e, low], lambda q: wide(gd, pair(q)), parent, 4, False)
        for a in range(3):
            rows = slice(128 * a, 128 * a + 128)
            keep = places[e][a][0] > 0
            off = jnp.where(keep, -acc3[e, rows], 0.0).astype(BF16)
            if e == 0:
                o3z[3 * r + a] = off
            else:
                o3f[c, rows] = off
            o3[e, a] = off
        if e == 0:
            ring_oz.begin()
        else:
            ring_o3.begin()

    base_sib = links.take(8)

    def update(who):
        both = dot(wt[...], o3f[who])
        for t in range(2):
            term[t, who] = both[:, t * 128 : t * 128 + 128].astype(BF16)
        at = base_sib + who
        links.start(term.at[1 - k, who], sib.at[who], at, at, other_core)

    update(c)
    ring_wt.both(4)
    for step in range(1, 5):
        ring_oz.both(step)
        ring_o3.both(step)
        update(wrap(c - step))
        if step < 4:
            update(wrap(c + step))
    for who in range(RING):
        links.arrived(sib.at[who], base_sib + who, other_core)

    def mine(who):
        return term[k, who].astype(F32) + sib[who].astype(F32)

    base_sum = links.take(8)

    def sum_step(step):
        for way in range(2):
            arm = 3 if way else 4
            if step > arm:
                continue
            apart = arm + 1 - step
            value = mine(wrap(z - apart) if way else wrap(z + apart))
            at = way * 4 + step - 1
            if step > 1:
                links.arrived(landed.at[at - 1], base_sum + at - 1, z_up)
                value = value + landed[at - 1].astype(F32)
            stage[at] = value.astype(BF16)
            device = z_down if way else z_up
            links.start(stage.at[at], landed.at[at], base_sum + at, base_sum + at, device)

    sum_step(1)

    finish_oz()
    sum_step(2)
    fold = lambda b: 3 * lax.bitwise_and(b, 15) + lax.shift_right_logical(b, 4)
    product(
        acc.at[top],
        lambda q: wide(wtt, four(q)),
        lambda q: jnp.concatenate([o3z[fold(lists[0, 4 * q + u])] for u in range(4)], axis=0),
        8,
    )
    base_move = links.take(4)
    for t in range(2):
        moved[t] = acc[top, t * 128 : t * 128 + 128].astype(BF16)
    stays = []
    for t in range(2):
        to = {"row": 2 * c + t, "col": z}
        made = links.copy(moved.at[t], arrived_at.at[k], base_move + t, base_move + 2 + k, to)
        own = (2 * c + t == r) & (z == c)
        local = pltpu.make_async_copy(moved.at[t], arrived_at.at[k], links.recv.at[base_move + 2 + k])
        pl.when(own)(local.start)
        pl.when(jnp.logical_not(own))(made.start)
        stays.append((own, made))
    sum_step(3)
    sum_step(4)
    loads['e3'].wait()
    rows256 = lax.broadcasted_iota(jnp.int32, (256, 128), 0)
    cols256 = lax.broadcasted_iota(jnp.int32, (256, 128), 1)

    def given_three(e):
        w3 = widths[NODES - BOTTOM + 2 * g + e]
        keep = (c * 256 + rows256 < w3) & (row_at + cols256 < w3)
        return jnp.where(keep, e3[e].astype(F32), 0.0)

    start = given_three(0)
    for t in range(2):
        links.arrived(arrived_at.at[t], base_move + 2 + t, other_core)
        rows = slice(t * 128, t * 128 + 128)
        d3[0, rows] = (start[rows] - arrived_at[t].astype(F32)).astype(BF16)
    total = mine(z)
    for way in range(2):
        at = 6 if way else 3
        links.arrived(landed.at[at], base_sum + at, z_up)
        total = total + landed[at].astype(F32)
    d3[1] = (given_three(1) - total).astype(BF16)
    links.drain()
    for wait in waits:
        wait()
    for own, made in stays:
        pl.when(jnp.logical_not(own))(made.wait_send)


def write_out(*refs):
    count = len(refs) // 2
    sems = refs[-1]
    copies = [
        pltpu.make_async_copy(refs[i], refs[count + i], sems.at[i]) for i in range(count)
    ]
    for one in copies:
        one.start()
    for one in copies:
        one.wait()


def local(widths, lists, root, p1, e1, p2, e2, p3, e3):
    vmem = pl.BlockSpec(memory_space=pltpu.VMEM)
    smem = pl.BlockSpec(memory_space=pltpu.SMEM)
    shapes = [(1, 128, 128), (1, 128, 128), (1, 2, 128, 256), (1, 256, 128), (2, 3, 128, 256), (2, 256, 128)]
    scratch = [
        ((2, 16, 128, 128), BF16),
        ((2, 128, 128), BF16),
        ((32, 128, 256), BF16),
        ((2, 32, 128, 256), BF16),
        ((32, 256, 128), BF16),
        ((8, 256, 256), BF16),
        ((32, 128, 128), BF16),
        ((8, 128, 256), BF16),
        ((2, 128, 128), BF16),
        ((2, 2, 128, 128), BF16),
        ((256, 256), F32),
        ((2, 384, 256), F32),
        ((8, 384, 256), BF16),
        ((256, 384), BF16),
        ((2, 8, 256, 128), BF16),
        ((8, 256, 128), BF16),
        ((8, 256, 128), BF16),
        ((8, 256, 128), BF16),
        ((48, 128, 256), BF16),
        ((32, 128, 128), BF16),
        ((2, 2, 128, 128), BF16),
        ((2, 128, 128), BF16),
        ((2, 128, 128), BF16),
        ((128, 2048), BF16),
        ((1, 128, 128), BF16),
        ((1, 128, 128), BF16),
        ((1, 2, 128, 256), BF16),
        ((1, 256, 128), BF16),
        ((2, 256, 256), BF16),
        ((2, 256, 128), BF16),
    ]
    hbm = pl.BlockSpec(memory_space=pltpu.HBM)
    made = pl.pallas_call(
        kernel,
        out_shape=[jax.ShapeDtypeStruct(shape, BF16) for shape in shapes],
        in_specs=[smem, smem] + [hbm] * 7,
        out_specs=[vmem] * 6,
        scratch_shapes=[pltpu.VMEM(*one) for one in scratch]
        + [pltpu.SemaphoreType.DMA((count,)) for count in (SEMS, SEMS, 7)],
        compiler_params=pltpu.CompilerParams(
            collective_id=0, has_side_effects=True, vmem_limit_bytes=VMEM
        ),
    )(widths, lists, root, p1, e1, p2, e2, p3, e3)
    return pl.pallas_call(
        write_out,
        out_shape=[jax.ShapeDtypeStruct(shape, BF16) for shape in shapes],
        in_specs=[vmem] * 6,
        out_specs=[hbm] * 6,
        scratch_shapes=[pltpu.SemaphoreType.DMA((6,))],
        compiler_params=pltpu.CompilerParams(vmem_limit_bytes=VMEM),
    )(*made)


def solution(mesh):
    in_specs = (
        P(),
        P("leaf", None),
        P("row", None),
        P("leaf", "row", "col"),
        P("leaf", "col", "row"),
        P("leaf", None, "row", "col"),
        P("leaf", "col", "row"),
        P("leaf", "row", "col"),
        P("leaf", "col", "row"),
    )
    out_specs = (
        P("leaf", "row", "col"),
        P("leaf", "col", "row"),
        P("leaf", None, "row", "col"),
        P("leaf", "col", "row"),
        P("leaf", None, "row", "col"),
        P("leaf", "col", "row"),
    )

    def whole(*args):
        return tuple(
            jax.shard_map(
                lambda *own: tuple(local(*own)),
                mesh=mesh,
                in_specs=in_specs,
                out_specs=out_specs,
                check_vma=False,
            )(*args)
        )

    return whole
```

```python
import jax
import jax.numpy as jnp
from jax import lax
from jax.experimental import pallas as pl
from jax.experimental.pallas import tpu as pltpu
from jax.sharding import PartitionSpec as P

NODES = 15
BOTTOM = 8
F32 = jnp.float32
BF16 = jnp.bfloat16
MESH = pl.DeviceIdType.MESH
SEMS = 384
VMEM = 63 * 1024 * 1024
RING = 8


def dot(a, b):
    return jnp.dot(a, b, preferred_element_type=F32)


def wrap(at):
    return lax.rem(at + 2 * RING, RING)


class Links:
    def __init__(self, send, recv):
        self.send, self.recv = send, recv
        self.used = 0
        self.sent = []

    def take(self, count):
        first = self.used
        self.used += count
        assert self.used <= SEMS
        return first

    def copy(self, src, dst, send_at, recv_at, device):
        return pltpu.make_async_remote_copy(
            src_ref=src,
            dst_ref=dst,
            send_sem=self.send.at[send_at],
            recv_sem=self.recv.at[recv_at],
            device_id=device,
            device_id_type=MESH,
        )

    def start(self, src, dst, send_at, recv_at, device):
        made = self.copy(src, dst, send_at, recv_at, device)
        made.start()
        self.sent.append(made)

    def arrived(self, ref, recv_at, device):
        self.copy(ref, ref, recv_at, recv_at, device).wait_recv()

    def drain(self):
        for made in self.sent:
            made.wait_send()


class Gather:
    def __init__(self, links, slot, me, up, down, heard=None):
        self.links, self.slot, self.me = links, slot, me
        self.up, self.down, self.heard = up, down, heard
        self.base = links.take(16)

    def sem(self, way, step, part):
        return self.base + way * 8 + (step - 1) * 2 + part

    def push(self, owner, way, step, part):
        ref = self.slot(owner, part)
        at = self.sem(way, step, part)
        self.links.start(ref, ref, at, at, self.down if way else self.up)

    def begin(self, parts=(0, 1)):
        for part in parts:
            self.push(self.me, 0, 1, part)
            self.push(self.me, 1, 1, part)
            if self.heard is not None:
                self.heard(self.me, part)

    def relay(self, step, part):
        for way in (part,) if step == 4 else (0, 1):
            owner = wrap(self.me + step) if way else wrap(self.me - step)
            self.links.arrived(self.slot(owner, part), self.sem(way, step, part), self.up)
            if step < 3 or (step == 3 and way == part):
                self.push(owner, way, step + 1, part)
            if self.heard is not None:
                self.heard(owner, part)

    def both(self, step):
        self.relay(step, 0)
        self.relay(step, 1)


def kernel(
    widths,
    lists,
    root_in,
    p1_in,
    e1_in,
    p2_in,
    e2_in,
    p3_in,
    e3_in,
    o1,
    d1,
    o2,
    d2,
    o3,
    d3,
    l1g,
    e1x,
    l2g,
    wg,
    ga,
    gb,
    gc,
    gd,
    ot1,
    ot2,
    acc,
    acc3,
    o3f,
    wt,
    term,
    sib,
    stage,
    landed,
    o3z,
    wtt,
    ot3,
    moved,
    arrived_at,
    root,
    p1,
    e1,
    p2,
    e2,
    p3,
    e3,
    send,
    recv,
    load_sem,
):
    g = lax.axis_index("leaf")
    r = lax.axis_index("row")
    c = lax.axis_index("col")
    z = lax.div(r, 2)
    k = lax.rem(r, 2)
    h = lax.rem(g, 2)
    links = Links(send, recv)
    waits = []
    z_up, z_down = {"row": lax.rem(r + 2, 16)}, {"row": lax.rem(r + 14, 16)}
    y_up, y_down = {"col": wrap(c + 1)}, {"col": wrap(c - 1)}
    other_core = {"row": r + 1 - 2 * k}
    other_leaf = {"leaf": g + 1 - 2 * h}

    barrier = pltpu.get_barrier_semaphore()
    greeted = [z_up, z_down, other_core, other_leaf] + [{"col": wrap(c + d)} for d in range(1, RING)]
    for device in greeted:
        pl.semaphore_signal(barrier, inc=1, device_id=device, device_id_type=MESH)
    loads = {}
    pairs = dict(
        p1=(p1_in, p1), root=(root_in, root), e1=(e1_in, e1), p2=(p2_in, p2),
        p3=(p3_in, p3), e2=(e2_in, e2), e3=(e3_in, e3),
    )
    for at, name in enumerate(pairs):
        loads[name] = pltpu.make_async_copy(*pairs[name], load_sem.at[at])
        loads[name].start()

    w0, w1, w2 = widths[0], widths[1 + lax.div(g, 2)], widths[3 + g]
    lane128 = lax.broadcasted_iota(jnp.int32, (128, 128), 1)
    row128 = lax.broadcasted_iota(jnp.int32, (128, 128), 0)
    lane256 = lax.broadcasted_iota(jnp.int32, (128, 256), 1)
    row_at = r * 128

    loads['p1'].wait()
    l1g[h, r] = jnp.where(h * 1024 + c * 128 + lane128 < w1, p1[0].astype(F32), 0.0).astype(BF16)
    loads['e1'].wait()
    pl.semaphore_wait(barrier, len(greeted))

    x_at = links.take(2)
    links.start(l1g.at[h, r], l1g.at[h, r], x_at, x_at, other_leaf)
    links.start(e1.at[0], e1x.at[h], x_at + 1, x_at + 1, other_leaf)

    def z_gather(slot):
        base = links.take(16)

        def heard(owner, part):
            ref = slot(2 * owner + k, part)
            at = base + owner * 2 + part
            links.start(ref, ref, at, at, other_core)

        def finish():
            for owner in range(RING):
                for part in range(2):
                    at = base + owner * 2 + part
                    links.arrived(slot(2 * owner + 1 - k, part), at, other_core)

        mine = lambda owner, part: slot(2 * owner + k, part)
        return Gather(links, mine, z, z_up, z_down, heard), finish

    def halves(part, size):
        return pl.ds(part * (size // 2), size // 2)

    def run(start, count):
        return pl.ds(pl.multiple_of(start, count), count)

    ring_l1, finish_l1 = z_gather(lambda who, part: l1g.at[1 - h if part else h, who])
    ring_l2, finish_l2 = z_gather(lambda who, part: l2g.at[2 * who + part])
    ring_w, finish_w = z_gather(lambda who, part: wg.at[part, run(2 * who, 2)])
    ring_oz, finish_oz = z_gather(lambda who, part: o3z.at[pl.ds(3 * who, 3), halves(part, 128)])

    ring_l1.begin((0,))
    links.arrived(l1g.at[1 - h, r], x_at, other_leaf)
    ring_l1.begin((1,))

    def mask_root(b, carry):
        cols = b * 128 + lane128
        keep = (row_at + row128 < w0) & (cols < w0)
        block = root[:, pl.ds(pl.multiple_of(b * 128, 128), 128)].astype(F32)
        ga[b, 0:128] = jnp.where(keep, block, 0.0).astype(BF16)
        return carry

    loads['root'].wait()
    lax.fori_loop(0, 16, mask_root, 0)
    own256 = c * 256 + lane256
    loads['p2'].wait()
    for part in range(2):
        l2g[2 * r + part] = jnp.where(own256 < w2, p2[0, part].astype(F32), 0.0).astype(BF16)
    ring_l1.both(1)
    ring_l1.both(2)
    ring_l2.begin()
    ring_l1.both(3)
    ring_l1.both(4)
    loads['p3'].wait()
    for e in range(2):
        w3 = widths[NODES - BOTTOM + 2 * g + e]
        for u in range(2):
            wg[e, 2 * r + u] = jnp.where(
                own256 < w3, p3[e, u * 128 : u * 128 + 128].astype(F32), 0.0
            ).astype(BF16)
    e1x[h] = e1[0]
    for u in range(2):
        for t in range(2):
            ot3[t, u] = wg[0, 2 * r + u, :, t * 128 : t * 128 + 128].astype(F32).T.astype(BF16)
    finish_l1()

    def product(target, lhs, rhs, count, fresh=True):
        if fresh:
            target[...] = jnp.zeros(target.shape, F32)

        def body(q, carry):
            target[...] += dot(lhs(q), rhs(q))
            return carry

        lax.fori_loop(0, count, body, 0)

    def wide(ref, blocks, rows=None):
        if rows is None:
            return jnp.concatenate([ref[b] for b in blocks], axis=1)
        return jnp.concatenate([ref[b, rows] for b in blocks], axis=1)

    def panel_one(q):
        return jnp.concatenate(
            [l1g[half, pl.ds(4 * q, 4)].reshape(512, 128) for half in range(2)], axis=1
        )

    top = slice(0, 128)
    mid = slice(128, 256)
    four = lambda q: [4 * q + u for u in range(4)]
    product(acc.at[top], lambda q: wide(ga, four(q), top), panel_one, 4)
    off = -acc[top]
    for half in range(2):
        block = off[:, half * 128 : half * 128 + 128]
        ga[16 + 2 * c + half, top] = block.astype(BF16)
        ot1[half] = block.T.astype(BF16)
    o1[0] = ga[16 + 2 * c + h, top]

    def sixteen(start, at):
        return pl.ds(pl.multiple_of(start + 16 * at, 16), 16)

    def turn(source, slot, dest_row):
        sends = links.take(16)
        first = links.take(16)
        for t in range(2):
            row_to = dest_row(t)
            for apart in range(RING):
                y = wrap(c + apart)
                src = source(t, y)
                dst = slot(r, y)
                at = sends + t * RING + apart
                made = links.copy(src, dst, at, first + r, {"row": row_to, "col": y})
                if apart == 0:
                    local = pltpu.make_async_copy(src, dst, links.recv.at[first + r])
                    pl.when(row_to == r)(local.start)
                    pl.when(row_to != r)(made.start)

                    def wait_made(made=made, row_to=row_to):
                        pl.when(row_to != r)(made.wait_send)

                    waits.append(wait_made)
                else:
                    made.start()
                    links.sent.append(made)

        def finish():
            for source_row in range(16):
                links.arrived(slot(source_row, c), first + source_row, y_up)

        return finish

    finish_t1 = turn(
        lambda t, y: ot1.at[t, sixteen(0, y)],
        lambda who, y: ga.at[who, sixteen(128, y)],
        lambda t: 8 * t + c,
    )
    y_gather = lambda slot: Gather(links, slot, c, y_up, y_down)
    ring_o1 = y_gather(
        lambda who, part: ga.at[16 + 2 * who + part, top]
    )
    ring_t1 = y_gather(lambda who, part: ga.at[halves(part, 16), sixteen(128, who)])
    ring_d1 = y_gather(
        lambda who, part: ga.at[16 + 2 * who + part, mid]
    )
    ring_o2 = y_gather(lambda who, part: gb.at[who, halves(part, 256)])
    ring_t2 = y_gather(lambda who, part: gc.at[halves(part, 32), sixteen(0, who)])
    ring_wt = y_gather(lambda who, part: wtt.at[halves(part, 32), sixteen(0, who)])
    ring_d2 = y_gather(lambda who, part: gd.at[who, halves(part, 128)])
    ring_o3 = y_gather(lambda who, part: o3f.at[who, halves(part, 384)])

    finish_t1()
    ring_t1.begin()
    ring_o1.begin()
    ring_l2.both(1)
    ring_t1.both(1)
    ring_l2.both(2)
    ring_t1.both(2)
    ring_t1.both(3)
    ring_o1.both(1)
    ring_t1.both(4)

    links.arrived(e1x.at[1 - h], x_at + 1, other_leaf)
    product(acc.at[top], lambda q: wide(ga, four(q), mid), panel_one, 4)
    for half in range(2):
        keep = (half * 1024 + c * 128 + lane128 < w1) & (row_at + row128 < w1)
        given = jnp.where(keep, e1x[half].astype(F32).T, 0.0)
        turned = given - acc[top, half * 128 : half * 128 + 128]
        ga[16 + 2 * c + half, mid] = turned.astype(BF16)
    ring_d1.begin()
    finish_t3 = turn(
        lambda t, y: ot3.at[t, :, sixteen(0, y)],
        lambda who, y: wtt.at[run(2 * who, 2), sixteen(0, y)],
        lambda t: 2 * c + t,
    )
    ring_l2.both(3)
    ring_o1.both(2)
    ring_d1.both(1)
    d1[0] = ga[16 + 2 * c + h, mid].astype(F32).T.astype(BF16)
    ring_l2.both(4)
    ring_w.begin()
    ring_o1.both(3)
    ring_d1.both(2)
    ring_d1.both(3)
    ring_o1.both(4)
    ring_d1.both(4)
    finish_l2()
    finish_t3()
    ring_wt.begin()

    panel_two = lambda q: l2g[pl.ds(4 * q, 4)].reshape(512, 256)
    second = lambda b: 16 + 2 * lax.bitwise_and(b, 7) + lax.shift_right_logical(b, 3)
    crossed = lambda q: [2 * q, second(2 * q), 2 * q + 1, second(2 * q + 1)]
    product(acc, lambda q: wide(ga, crossed(q)), panel_two, 8)
    for a in range(2):
        rows = slice(128 * a, 128 * a + 128)
        off = -acc[rows]
        gb[c, rows] = off.astype(BF16)
        for t in range(2):
            ot2[t, a] = off[:, t * 128 : t * 128 + 128].T.astype(BF16)
    finish_t2 = turn(
        lambda t, y: ot2.at[t, :, sixteen(0, y)],
        lambda who, y: gc.at[pl.ds(pl.multiple_of(2 * who, 2), 2), sixteen(0, y)],
        lambda t: 2 * c + t,
    )
    for a in range(2):
        o2[0, a] = gb[c, 128 * a : 128 * a + 128]
    ring_w.both(1)
    ring_wt.both(1)
    finish_t2()
    ring_t2.begin()
    ring_o2.begin()
    ring_w.both(2)
    ring_t2.both(1)
    ring_t2.both(2)
    ring_w.both(3)
    ring_t2.both(3)
    ring_o2.both(1)
    ring_t2.both(4)

    loads['e2'].wait()
    product(acc.at[top], lambda q: wide(gc, four(q)), panel_two, 8)
    for half in range(2):
        cols = slice(half * 128, half * 128 + 128)
        keep = (c * 256 + half * 128 + lane128 < w2) & (row_at + row128 < w2)
        given = jnp.where(keep, e2[0, cols].astype(F32).T, 0.0)
        turned = (given - acc[top, cols]).astype(BF16)
        gd[c, :, cols] = turned
        d2[0, cols] = turned.astype(F32).T.astype(BF16)
    ring_d2.begin()
    ring_w.both(4)
    ring_wt.both(2)
    ring_o2.both(2)
    ring_d2.both(1)
    ring_o2.both(3)
    ring_d2.both(2)
    ring_d2.both(3)
    ring_o2.both(4)
    ring_wt.both(3)
    finish_w()

    low = slice(256, 384)
    def placed(b):
        return jnp.where(b < 16, b, second(lax.bitwise_and(b, 15)))

    def paired(b):
        return 2 * lax.bitwise_and(b, 15) + lax.shift_right_logical(b, 4)

    for e in range(2):
        panel = lambda q, e=e: wg[e, pl.ds(4 * q, 4)].reshape(512, 256)
        listed = lambda q, e=e: [lists[e, 4 * q + u] for u in range(4)]
        product(acc3.at[e, 0:256], lambda q: wide(ga, [placed(b) for b in listed(q)]), panel, 4)
        product(acc3.at[e, low], lambda q: wide(gc, [paired(b) for b in listed(q)]), panel, 4)
    places = []
    for e in range(2):
        row = []
        for a in range(2):
            found, where = jnp.int32(0), jnp.int32(0)
            for i in range(16):
                hit = lists[e, i] == 16 * a + r
                found, where = jnp.where(hit, 1, found), jnp.where(hit, i, where)
            row.append((found, where))
        row.append((jnp.int32(1), 16 + r))
        places.append(row)
        for a in range(3):
            if e == 1:
                wt[:, 128 * a : 128 * a + 128] = wg[e, row[a][1]].astype(F32).T.astype(BF16)
    ring_d2.both(4)
    for e in range(2):
        parent = lambda q, e=e: wg[e, pl.ds(16 + 4 * q, 4)].reshape(512, 256)
        pair = lambda q: [2 * q, 2 * q + 1]
        product(acc3.at[e, 0:256], lambda q: wide(gb, pair(q)), parent, 4, False)
        product(acc3.at[e, low], lambda q: wide(gd, pair(q)), parent, 4, False)
        for a in range(3):
            rows = slice(128 * a, 128 * a + 128)
            keep = places[e][a][0] > 0
            off = jnp.where(keep, -acc3[e, rows], 0.0).astype(BF16)
            if e == 0:
                o3z[3 * r + a] = off
            else:
                o3f[c, rows] = off
            o3[e, a] = off
        if e == 0:
            ring_oz.begin()
        else:
            ring_o3.begin()

    base_sib = links.take(8)

    def update(who):
        both = dot(wt[...], o3f[who])
        for t in range(2):
            term[t, who] = both[:, t * 128 : t * 128 + 128].astype(BF16)
        at = base_sib + who
        links.start(term.at[1 - k, who], sib.at[who], at, at, other_core)

    update(c)
    ring_wt.both(4)
    for step in range(1, 5):
        ring_oz.both(step)
        ring_o3.both(step)
        update(wrap(c - step))
        if step < 4:
            update(wrap(c + step))
    for who in range(RING):
        links.arrived(sib.at[who], base_sib + who, other_core)

    def mine(who):
        return term[k, who].astype(F32) + sib[who].astype(F32)

    base_sum = links.take(8)

    def sum_step(step):
        for way in range(2):
            arm = 3 if way else 4
            if step > arm:
                continue
            apart = arm + 1 - step
            value = mine(wrap(z - apart) if way else wrap(z + apart))
            at = way * 4 + step - 1
            if step > 1:
                links.arrived(landed.at[at - 1], base_sum + at - 1, z_up)
                value = value + landed[at - 1].astype(F32)
            stage[at] = value.astype(BF16)
            device = z_down if way else z_up
            links.start(stage.at[at], landed.at[at], base_sum + at, base_sum + at, device)

    sum_step(1)

    finish_oz()
    sum_step(2)
    fold = lambda b: 3 * lax.bitwise_and(b, 15) + lax.shift_right_logical(b, 4)
    product(
        acc.at[top],
        lambda q: wide(wtt, four(q)),
        lambda q: jnp.concatenate([o3z[fold(lists[0, 4 * q + u])] for u in range(4)], axis=0),
        8,
    )
    base_move = links.take(4)
    for t in range(2):
        moved[t] = acc[top, t * 128 : t * 128 + 128].astype(BF16)
    stays = []
    for t in range(2):
        to = {"row": 2 * c + t, "col": z}
        made = links.copy(moved.at[t], arrived_at.at[k], base_move + t, base_move + 2 + k, to)
        own = (2 * c + t == r) & (z == c)
        local = pltpu.make_async_copy(moved.at[t], arrived_at.at[k], links.recv.at[base_move + 2 + k])
        pl.when(own)(local.start)
        pl.when(jnp.logical_not(own))(made.start)
        stays.append((own, made))
    sum_step(3)
    sum_step(4)
    loads['e3'].wait()
    rows256 = lax.broadcasted_iota(jnp.int32, (256, 128), 0)
    cols256 = lax.broadcasted_iota(jnp.int32, (256, 128), 1)

    def given_three(e):
        w3 = widths[NODES - BOTTOM + 2 * g + e]
        keep = (c * 256 + rows256 < w3) & (row_at + cols256 < w3)
        return jnp.where(keep, e3[e].astype(F32), 0.0)

    start = given_three(0)
    for t in range(2):
        links.arrived(arrived_at.at[t], base_move + 2 + t, other_core)
        rows = slice(t * 128, t * 128 + 128)
        d3[0, rows] = (start[rows] - arrived_at[t].astype(F32)).astype(BF16)
    total = mine(z)
    for way in range(2):
        at = 6 if way else 3
        links.arrived(landed.at[at], base_sum + at, z_up)
        total = total + landed[at].astype(F32)
    d3[1] = (given_three(1) - total).astype(BF16)
    links.drain()
    for wait in waits:
        wait()
    for own, made in stays:
        pl.when(jnp.logical_not(own))(made.wait_send)


def write_out(*refs):
    count = len(refs) // 2
    sems = refs[-1]
    copies = [
        pltpu.make_async_copy(refs[i], refs[count + i], sems.at[i]) for i in range(count)
    ]
    for one in copies:
        one.start()
    for one in copies:
        one.wait()


def local(widths, lists, root, p1, e1, p2, e2, p3, e3):
    vmem = pl.BlockSpec(memory_space=pltpu.VMEM)
    smem = pl.BlockSpec(memory_space=pltpu.SMEM)
    shapes = [(1, 128, 128), (1, 128, 128), (1, 2, 128, 256), (1, 256, 128), (2, 3, 128, 256), (2, 256, 128)]
    scratch = [
        ((2, 16, 128, 128), BF16),
        ((2, 128, 128), BF16),
        ((32, 128, 256), BF16),
        ((2, 32, 128, 256), BF16),
        ((32, 256, 128), BF16),
        ((8, 256, 256), BF16),
        ((32, 128, 128), BF16),
        ((8, 128, 256), BF16),
        ((2, 128, 128), BF16),
        ((2, 2, 128, 128), BF16),
        ((256, 256), F32),
        ((2, 384, 256), F32),
        ((8, 384, 256), BF16),
        ((256, 384), BF16),
        ((2, 8, 256, 128), BF16),
        ((8, 256, 128), BF16),
        ((8, 256, 128), BF16),
        ((8, 256, 128), BF16),
        ((48, 128, 256), BF16),
        ((32, 128, 128), BF16),
        ((2, 2, 128, 128), BF16),
        ((2, 128, 128), BF16),
        ((2, 128, 128), BF16),
        ((128, 2048), BF16),
        ((1, 128, 128), BF16),
        ((1, 128, 128), BF16),
        ((1, 2, 128, 256), BF16),
        ((1, 256, 128), BF16),
        ((2, 256, 256), BF16),
        ((2, 256, 128), BF16),
    ]
    hbm = pl.BlockSpec(memory_space=pltpu.HBM)
    made = pl.pallas_call(
        kernel,
        out_shape=[jax.ShapeDtypeStruct(shape, BF16) for shape in shapes],
        in_specs=[smem, smem] + [hbm] * 7,
        out_specs=[vmem] * 6,
        scratch_shapes=[pltpu.VMEM(*one) for one in scratch]
        + [pltpu.SemaphoreType.DMA((count,)) for count in (SEMS, SEMS, 7)],
        compiler_params=pltpu.CompilerParams(
            collective_id=0, has_side_effects=True, vmem_limit_bytes=VMEM
        ),
    )(widths, lists, root, p1, e1, p2, e2, p3, e3)
    return pl.pallas_call(
        write_out,
        out_shape=[jax.ShapeDtypeStruct(shape, BF16) for shape in shapes],
        in_specs=[vmem] * 6,
        out_specs=[hbm] * 6,
        scratch_shapes=[pltpu.SemaphoreType.DMA((6,))],
        compiler_params=pltpu.CompilerParams(vmem_limit_bytes=VMEM),
    )(*made)


def solution(mesh):
    in_specs = (
        P(),
        P("leaf", None),
        P("row", None),
        P("leaf", "row", "col"),
        P("leaf", "col", "row"),
        P("leaf", None, "row", "col"),
        P("leaf", "col", "row"),
        P("leaf", "row", "col"),
        P("leaf", "col", "row"),
    )
    out_specs = (
        P("leaf", "row", "col"),
        P("leaf", "col", "row"),
        P("leaf", None, "row", "col"),
        P("leaf", "col", "row"),
        P("leaf", None, "row", "col"),
        P("leaf", "col", "row"),
    )

    def whole(*args):
        return tuple(
            jax.shard_map(
                lambda *own: tuple(local(*own)),
                mesh=mesh,
                in_specs=in_specs,
                out_specs=out_specs,
                check_vma=False,
            )(*args)
        )

    return whole
```

```python
import jax
import jax.numpy as jnp
from jax import lax
from jax.experimental import pallas as pl
from jax.experimental.pallas import tpu as pltpu
from jax.sharding import PartitionSpec as P

NODES = 15
BOTTOM = 8
F32 = jnp.float32
BF16 = jnp.bfloat16
MESH = pl.DeviceIdType.MESH
SEMS = 384
VMEM = 63 * 1024 * 1024
RING = 8


def dot(a, b):
    return jnp.dot(a, b, preferred_element_type=F32)


def wrap(at):
    return lax.rem(at + 2 * RING, RING)


class Links:
    def __init__(self, send, recv):
        self.send, self.recv = send, recv
        self.used = 0
        self.sent = []

    def take(self, count):
        first = self.used
        self.used += count
        assert self.used <= SEMS
        return first

    def copy(self, src, dst, send_at, recv_at, device):
        return pltpu.make_async_remote_copy(
            src_ref=src,
            dst_ref=dst,
            send_sem=self.send.at[send_at],
            recv_sem=self.recv.at[recv_at],
            device_id=device,
            device_id_type=MESH,
        )

    def start(self, src, dst, send_at, recv_at, device):
        made = self.copy(src, dst, send_at, recv_at, device)
        made.start()
        self.sent.append(made)

    def arrived(self, ref, recv_at, device):
        self.copy(ref, ref, recv_at, recv_at, device).wait_recv()

    def drain(self):
        for made in self.sent:
            made.wait_send()


class Gather:
    def __init__(self, links, slot, me, up, down, heard=None):
        self.links, self.slot, self.me = links, slot, me
        self.up, self.down, self.heard = up, down, heard
        self.base = links.take(16)

    def sem(self, way, step, part):
        return self.base + way * 8 + (step - 1) * 2 + part

    def push(self, owner, way, step, part):
        ref = self.slot(owner, part)
        at = self.sem(way, step, part)
        self.links.start(ref, ref, at, at, self.down if way else self.up)

    def begin(self, parts=(0, 1)):
        for part in parts:
            self.push(self.me, 0, 1, part)
            self.push(self.me, 1, 1, part)
            if self.heard is not None:
                self.heard(self.me, part)

    def relay(self, step, part):
        for way in (part,) if step == 4 else (0, 1):
            owner = wrap(self.me + step) if way else wrap(self.me - step)
            self.links.arrived(self.slot(owner, part), self.sem(way, step, part), self.up)
            if step < 3 or (step == 3 and way == part):
                self.push(owner, way, step + 1, part)
            if self.heard is not None:
                self.heard(owner, part)

    def both(self, step):
        self.relay(step, 0)
        self.relay(step, 1)


def kernel(
    widths,
    lists,
    root_in,
    p1_in,
    e1_in,
    p2_in,
    e2_in,
    p3_in,
    e3_in,
    o1,
    d1,
    o2,
    d2,
    o3,
    d3,
    l1g,
    e1x,
    l2g,
    wg,
    ga,
    gb,
    gc,
    gd,
    ot1,
    ot2,
    acc,
    acc3,
    o3f,
    wt,
    term,
    sib,
    stage,
    landed,
    o3z,
    wtt,
    ot3,
    moved,
    arrived_at,
    root,
    p1,
    e1,
    p2,
    e2,
    p3,
    e3,
    send,
    recv,
    load_sem,
):
    g = lax.axis_index("leaf")
    r = lax.axis_index("row")
    c = lax.axis_index("col")
    z = lax.div(r, 2)
    k = lax.rem(r, 2)
    h = lax.rem(g, 2)
    links = Links(send, recv)
    waits = []
    z_up, z_down = {"row": lax.rem(r + 2, 16)}, {"row": lax.rem(r + 14, 16)}
    y_up, y_down = {"col": wrap(c + 1)}, {"col": wrap(c - 1)}
    other_core = {"row": r + 1 - 2 * k}
    other_leaf = {"leaf": g + 1 - 2 * h}

    barrier = pltpu.get_barrier_semaphore()
    greeted = [z_up, z_down, other_core, other_leaf] + [{"col": wrap(c + d)} for d in range(1, RING)]
    for device in greeted:
        pl.semaphore_signal(barrier, inc=1, device_id=device, device_id_type=MESH)
    loads = {}
    pairs = dict(
        p1=(p1_in, p1), root=(root_in, root), e1=(e1_in, e1), p2=(p2_in, p2),
        p3=(p3_in, p3), e2=(e2_in, e2), e3=(e3_in, e3),
    )
    for at, name in enumerate(pairs):
        loads[name] = pltpu.make_async_copy(*pairs[name], load_sem.at[at])
        loads[name].start()

    w0, w1, w2 = widths[0], widths[1 + lax.div(g, 2)], widths[3 + g]
    lane128 = lax.broadcasted_iota(jnp.int32, (128, 128), 1)
    row128 = lax.broadcasted_iota(jnp.int32, (128, 128), 0)
    lane256 = lax.broadcasted_iota(jnp.int32, (128, 256), 1)
    row_at = r * 128

    loads['p1'].wait()
    l1g[h, r] = jnp.where(h * 1024 + c * 128 + lane128 < w1, p1[0].astype(F32), 0.0).astype(BF16)
    loads['e1'].wait()
    pl.semaphore_wait(barrier, len(greeted))

    x_at = links.take(2)
    links.start(l1g.at[h, r], l1g.at[h, r], x_at, x_at, other_leaf)
    links.start(e1.at[0], e1x.at[h], x_at + 1, x_at + 1, other_leaf)

    def z_gather(slot):
        base = links.take(16)

        def heard(owner, part):
            ref = slot(2 * owner + k, part)
            at = base + owner * 2 + part
            links.start(ref, ref, at, at, other_core)

        def finish():
            for owner in range(RING):
                for part in range(2):
                    at = base + owner * 2 + part
                    links.arrived(slot(2 * owner + 1 - k, part), at, other_core)

        mine = lambda owner, part: slot(2 * owner + k, part)
        return Gather(links, mine, z, z_up, z_down, heard), finish

    def halves(part, size):
        return pl.ds(part * (size // 2), size // 2)

    def run(start, count):
        return pl.ds(pl.multiple_of(start, count), count)

    ring_l1, finish_l1 = z_gather(lambda who, part: l1g.at[1 - h if part else h, who])
    ring_l2, finish_l2 = z_gather(lambda who, part: l2g.at[2 * who + part])
    ring_w, finish_w = z_gather(lambda who, part: wg.at[part, run(2 * who, 2)])
    ring_oz, finish_oz = z_gather(lambda who, part: o3z.at[pl.ds(3 * who, 3), halves(part, 128)])

    ring_l1.begin((0,))
    links.arrived(l1g.at[1 - h, r], x_at, other_leaf)
    ring_l1.begin((1,))

    def mask_root(b, carry):
        cols = b * 128 + lane128
        keep = (row_at + row128 < w0) & (cols < w0)
        block = root[:, pl.ds(pl.multiple_of(b * 128, 128), 128)].astype(F32)
        ga[b, 0:128] = jnp.where(keep, block, 0.0).astype(BF16)
        return carry

    loads['root'].wait()
    lax.fori_loop(0, 16, mask_root, 0)
    own256 = c * 256 + lane256
    loads['p2'].wait()
    for part in range(2):
        l2g[2 * r + part] = jnp.where(own256 < w2, p2[0, part].astype(F32), 0.0).astype(BF16)
    ring_l1.both(1)
    ring_l1.both(2)
    ring_l2.begin()
    ring_l1.both(3)
    ring_l1.both(4)
    loads['p3'].wait()
    for e in range(2):
        w3 = widths[NODES - BOTTOM + 2 * g + e]
        for u in range(2):
            wg[e, 2 * r + u] = jnp.where(
                own256 < w3, p3[e, u * 128 : u * 128 + 128].astype(F32), 0.0
            ).astype(BF16)
    e1x[h] = e1[0]
    for u in range(2):
        for t in range(2):
            ot3[t, u] = wg[0, 2 * r + u, :, t * 128 : t * 128 + 128].astype(F32).T.astype(BF16)
    finish_l1()

    def product(target, lhs, rhs, count, fresh=True):
        if fresh:
            target[...] = jnp.zeros(target.shape, F32)

        def body(q, carry):
            target[...] += dot(lhs(q), rhs(q))
            return carry

        lax.fori_loop(0, count, body, 0)

    def wide(ref, blocks, rows=None):
        if rows is None:
            return jnp.concatenate([ref[b] for b in blocks], axis=1)
        return jnp.concatenate([ref[b, rows] for b in blocks], axis=1)

    def panel_one(q):
        return jnp.concatenate(
            [l1g[half, pl.ds(4 * q, 4)].reshape(512, 128) for half in range(2)], axis=1
        )

    top = slice(0, 128)
    mid = slice(128, 256)
    four = lambda q: [4 * q + u for u in range(4)]
    product(acc.at[top], lambda q: wide(ga, four(q), top), panel_one, 4)
    off = -acc[top]
    for half in range(2):
        block = off[:, half * 128 : half * 128 + 128]
        ga[16 + 2 * c + half, top] = block.astype(BF16)
        ot1[half] = block.T.astype(BF16)
    o1[0] = ga[16 + 2 * c + h, top]

    def sixteen(start, at):
        return pl.ds(pl.multiple_of(start + 16 * at, 16), 16)

    def turn(source, slot, dest_row):
        sends = links.take(16)
        first = links.take(16)
        for t in range(2):
            row_to = dest_row(t)
            for apart in range(RING):
                y = wrap(c + apart)
                src = source(t, y)
                dst = slot(r, y)
                at = sends + t * RING + apart
                made = links.copy(src, dst, at, first + r, {"row": row_to, "col": y})
                if apart == 0:
                    local = pltpu.make_async_copy(src, dst, links.recv.at[first + r])
                    pl.when(row_to == r)(local.start)
                    pl.when(row_to != r)(made.start)

                    def wait_made(made=made, row_to=row_to):
                        pl.when(row_to != r)(made.wait_send)

                    waits.append(wait_made)
                else:
                    made.start()
                    links.sent.append(made)

        def finish():
            for source_row in range(16):
                links.arrived(slot(source_row, c), first + source_row, y_up)

        return finish

    finish_t1 = turn(
        lambda t, y: ot1.at[t, sixteen(0, y)],
        lambda who, y: ga.at[who, sixteen(128, y)],
        lambda t: 8 * t + c,
    )
    y_gather = lambda slot: Gather(links, slot, c, y_up, y_down)
    ring_o1 = y_gather(
        lambda who, part: ga.at[16 + 2 * who + part, top]
    )
    ring_t1 = y_gather(lambda who, part: ga.at[halves(part, 16), sixteen(128, who)])
    ring_d1 = y_gather(
        lambda who, part: ga.at[16 + 2 * who + part, mid]
    )
    ring_o2 = y_gather(lambda who, part: gb.at[who, halves(part, 256)])
    ring_t2 = y_gather(lambda who, part: gc.at[halves(part, 32), sixteen(0, who)])
    ring_wt = y_gather(lambda who, part: wtt.at[halves(part, 32), sixteen(0, who)])
    ring_d2 = y_gather(lambda who, part: gd.at[who, halves(part, 128)])
    ring_o3 = y_gather(lambda who, part: o3f.at[who, halves(part, 384)])

    finish_t1()
    ring_t1.begin()
    ring_o1.begin()
    ring_l2.both(1)
    ring_t1.both(1)
    ring_o1.both(1)
    ring_l2.both(2)
    ring_t1.both(2)
    ring_o1.both(2)
    ring_t1.both(3)
    ring_o1.both(3)
    ring_t1.both(4)
    ring_o1.both(4)

    links.arrived(e1x.at[1 - h], x_at + 1, other_leaf)
    product(acc.at[top], lambda q: wide(ga, four(q), mid), panel_one, 4)
    for half in range(2):
        keep = (half * 1024 + c * 128 + lane128 < w1) & (row_at + row128 < w1)
        given = jnp.where(keep, e1x[half].astype(F32).T, 0.0)
        turned = given - acc[top, half * 128 : half * 128 + 128]
        ga[16 + 2 * c + half, mid] = turned.astype(BF16)
    ring_d1.begin()
    finish_t3 = turn(
        lambda t, y: ot3.at[t, :, sixteen(0, y)],
        lambda who, y: wtt.at[run(2 * who, 2), sixteen(0, y)],
        lambda t: 2 * c + t,
    )
    ring_l2.both(3)
    ring_d1.both(1)
    d1[0] = ga[16 + 2 * c + h, mid].astype(F32).T.astype(BF16)
    ring_l2.both(4)
    ring_w.begin()
    ring_d1.both(2)
    ring_d1.both(3)
    ring_d1.both(4)
    finish_l2()
    finish_t3()
    ring_wt.begin()

    panel_two = lambda q: l2g[pl.ds(4 * q, 4)].reshape(512, 256)
    second = lambda b: 16 + 2 * lax.bitwise_and(b, 7) + lax.shift_right_logical(b, 3)
    crossed = lambda q: [2 * q, second(2 * q), 2 * q + 1, second(2 * q + 1)]
    product(acc, lambda q: wide(ga, crossed(q)), panel_two, 8)
    for a in range(2):
        rows = slice(128 * a, 128 * a + 128)
        off = -acc[rows]
        gb[c, rows] = off.astype(BF16)
        for t in range(2):
            ot2[t, a] = off[:, t * 128 : t * 128 + 128].T.astype(BF16)
    finish_t2 = turn(
        lambda t, y: ot2.at[t, :, sixteen(0, y)],
        lambda who, y: gc.at[pl.ds(pl.multiple_of(2 * who, 2), 2), sixteen(0, y)],
        lambda t: 2 * c + t,
    )
    for a in range(2):
        o2[0, a] = gb[c, 128 * a : 128 * a + 128]
    ring_w.both(1)
    ring_wt.both(1)
    finish_t2()
    ring_t2.begin()
    ring_o2.begin()
    ring_w.both(2)
    ring_t2.both(1)
    ring_o2.both(1)
    ring_t2.both(2)
    ring_o2.both(2)
    ring_w.both(3)
    ring_t2.both(3)
    ring_o2.both(3)
    ring_t2.both(4)
    ring_o2.both(4)

    loads['e2'].wait()
    product(acc.at[top], lambda q: wide(gc, four(q)), panel_two, 8)
    for half in range(2):
        cols = slice(half * 128, half * 128 + 128)
        keep = (c * 256 + half * 128 + lane128 < w2) & (row_at + row128 < w2)
        given = jnp.where(keep, e2[0, cols].astype(F32).T, 0.0)
        turned = (given - acc[top, cols]).astype(BF16)
        gd[c, :, cols] = turned
        d2[0, cols] = turned.astype(F32).T.astype(BF16)
    ring_d2.begin()
    ring_d2.both(1)
    ring_w.both(4)
    ring_d2.both(2)
    ring_wt.both(2)
    ring_d2.both(3)
    ring_wt.both(3)
    finish_w()

    low = slice(256, 384)
    def placed(b):
        return jnp.where(b < 16, b, second(lax.bitwise_and(b, 15)))

    def paired(b):
        return 2 * lax.bitwise_and(b, 15) + lax.shift_right_logical(b, 4)

    acc3[...] = jnp.zeros(acc3.shape, F32)

    def above(at, carry):
        e, q = lax.div(at, 4), lax.rem(at, 4)
        panel = wg[e, pl.ds(4 * q, 4)].reshape(512, 256)
        listed = [lists[e, 4 * q + u] for u in range(4)]
        acc3[e, 0:256] += dot(wide(ga, [placed(b) for b in listed]), panel)
        acc3[e, low] += dot(wide(gc, [paired(b) for b in listed]), panel)
        return carry

    lax.fori_loop(0, 8, above, 0)
    places = []
    for e in range(2):
        row = []
        for a in range(2):
            found, where = jnp.int32(0), jnp.int32(0)
            for i in range(16):
                hit = lists[e, i] == 16 * a + r
                found, where = jnp.where(hit, 1, found), jnp.where(hit, i, where)
            row.append((found, where))
        row.append((jnp.int32(1), 16 + r))
        places.append(row)
        for a in range(3):
            if e == 1:
                wt[:, 128 * a : 128 * a + 128] = wg[e, row[a][1]].astype(F32).T.astype(BF16)
    ring_d2.both(4)

    def beside(at, carry):
        e, q = lax.div(at, 4), lax.rem(at, 4)
        panel = wg[e, pl.ds(16 + 4 * q, 4)].reshape(512, 256)
        acc3[e, 0:256] += dot(wide(gb, [2 * q, 2 * q + 1]), panel)
        acc3[e, low] += dot(wide(gd, [2 * q, 2 * q + 1]), panel)
        return carry

    for e in range(2):
        lax.fori_loop(4 * e, 4 * e + 4, beside, 0)
        for a in range(3):
            rows = slice(128 * a, 128 * a + 128)
            keep = places[e][a][0] > 0
            off = jnp.where(keep, -acc3[e, rows], 0.0).astype(BF16)
            if e == 0:
                o3z[3 * r + a] = off
            else:
                o3f[c, rows] = off
            o3[e, a] = off
        if e == 0:
            ring_oz.begin()
        else:
            ring_o3.begin()

    base_sib = links.take(8)

    def shared(who):
        return links.copy(
            term.at[1 - k, who], sib.at[who], base_sib + who, base_sib + who, other_core
        )

    def update(who, carry):
        both = dot(wt[...], o3f[who])
        for t in range(2):
            term[t, who] = both[:, t * 128 : t * 128 + 128].astype(BF16)
        shared(who).start()
        return carry

    def passed(who, carry):
        shared(who).wait_send()
        return carry

    ring_wt.both(4)
    for step in range(1, 5):
        ring_oz.both(step)
        ring_o3.both(step)
    lax.fori_loop(0, RING, update, 0)
    for who in range(RING):
        links.arrived(sib.at[who], base_sib + who, other_core)

    def mine(who):
        return term[k, who].astype(F32) + sib[who].astype(F32)

    base_sum = links.take(8)

    def sum_step(step):
        for way in range(2):
            arm = 3 if way else 4
            if step > arm:
                continue
            apart = arm + 1 - step
            value = mine(wrap(z - apart) if way else wrap(z + apart))
            at = way * 4 + step - 1
            if step > 1:
                links.arrived(landed.at[at - 1], base_sum + at - 1, z_up)
                value = value + landed[at - 1].astype(F32)
            stage[at] = value.astype(BF16)
            device = z_down if way else z_up
            links.start(stage.at[at], landed.at[at], base_sum + at, base_sum + at, device)

    sum_step(1)

    finish_oz()
    sum_step(2)
    fold = lambda b: 3 * lax.bitwise_and(b, 15) + lax.shift_right_logical(b, 4)
    product(
        acc.at[top],
        lambda q: wide(wtt, four(q)),
        lambda q: jnp.concatenate([o3z[fold(lists[0, 4 * q + u])] for u in range(4)], axis=0),
        8,
    )
    base_move = links.take(4)
    for t in range(2):
        moved[t] = acc[top, t * 128 : t * 128 + 128].astype(BF16)
    stays = []
    for t in range(2):
        to = {"row": 2 * c + t, "col": z}
        made = links.copy(moved.at[t], arrived_at.at[k], base_move + t, base_move + 2 + k, to)
        own = (2 * c + t == r) & (z == c)
        local = pltpu.make_async_copy(moved.at[t], arrived_at.at[k], links.recv.at[base_move + 2 + k])
        pl.when(own)(local.start)
        pl.when(jnp.logical_not(own))(made.start)
        stays.append((own, made))
    sum_step(3)
    sum_step(4)
    loads['e3'].wait()
    rows256 = lax.broadcasted_iota(jnp.int32, (256, 128), 0)
    cols256 = lax.broadcasted_iota(jnp.int32, (256, 128), 1)

    def given_three(e):
        w3 = widths[NODES - BOTTOM + 2 * g + e]
        keep = (c * 256 + rows256 < w3) & (row_at + cols256 < w3)
        return jnp.where(keep, e3[e].astype(F32), 0.0)

    start = given_three(0)
    for t in range(2):
        links.arrived(arrived_at.at[t], base_move + 2 + t, other_core)
        rows = slice(t * 128, t * 128 + 128)
        d3[0, rows] = (start[rows] - arrived_at[t].astype(F32)).astype(BF16)
    total = mine(z)
    for way in range(2):
        at = 6 if way else 3
        links.arrived(landed.at[at], base_sum + at, z_up)
        total = total + landed[at].astype(F32)
    d3[1] = (given_three(1) - total).astype(BF16)
    links.drain()
    lax.fori_loop(0, RING, passed, 0)
    for wait in waits:
        wait()
    for own, made in stays:
        pl.when(jnp.logical_not(own))(made.wait_send)


def write_out(*refs):
    count = len(refs) // 2
    sems = refs[-1]
    copies = [
        pltpu.make_async_copy(refs[i], refs[count + i], sems.at[i]) for i in range(count)
    ]
    for one in copies:
        one.start()
    for one in copies:
        one.wait()


def local(widths, lists, root, p1, e1, p2, e2, p3, e3):
    vmem = pl.BlockSpec(memory_space=pltpu.VMEM)
    smem = pl.BlockSpec(memory_space=pltpu.SMEM)
    shapes = [(1, 128, 128), (1, 128, 128), (1, 2, 128, 256), (1, 256, 128), (2, 3, 128, 256), (2, 256, 128)]
    scratch = [
        ((2, 16, 128, 128), BF16),
        ((2, 128, 128), BF16),
        ((32, 128, 256), BF16),
        ((2, 32, 128, 256), BF16),
        ((32, 256, 128), BF16),
        ((8, 256, 256), BF16),
        ((32, 128, 128), BF16),
        ((8, 128, 256), BF16),
        ((2, 128, 128), BF16),
        ((2, 2, 128, 128), BF16),
        ((256, 256), F32),
        ((2, 384, 256), F32),
        ((8, 384, 256), BF16),
        ((256, 384), BF16),
        ((2, 8, 256, 128), BF16),
        ((8, 256, 128), BF16),
        ((8, 256, 128), BF16),
        ((8, 256, 128), BF16),
        ((48, 128, 256), BF16),
        ((32, 128, 128), BF16),
        ((2, 2, 128, 128), BF16),
        ((2, 128, 128), BF16),
        ((2, 128, 128), BF16),
        ((128, 2048), BF16),
        ((1, 128, 128), BF16),
        ((1, 128, 128), BF16),
        ((1, 2, 128, 256), BF16),
        ((1, 256, 128), BF16),
        ((2, 256, 256), BF16),
        ((2, 256, 128), BF16),
    ]
    hbm = pl.BlockSpec(memory_space=pltpu.HBM)
    made = pl.pallas_call(
        kernel,
        out_shape=[jax.ShapeDtypeStruct(shape, BF16) for shape in shapes],
        in_specs=[smem, smem] + [hbm] * 7,
        out_specs=[vmem] * 6,
        scratch_shapes=[pltpu.VMEM(*one) for one in scratch]
        + [pltpu.SemaphoreType.DMA((count,)) for count in (SEMS, SEMS, 7)],
        compiler_params=pltpu.CompilerParams(
            collective_id=0, has_side_effects=True, vmem_limit_bytes=VMEM
        ),
    )(widths, lists, root, p1, e1, p2, e2, p3, e3)
    return pl.pallas_call(
        write_out,
        out_shape=[jax.ShapeDtypeStruct(shape, BF16) for shape in shapes],
        in_specs=[vmem] * 6,
        out_specs=[hbm] * 6,
        scratch_shapes=[pltpu.SemaphoreType.DMA((6,))],
        compiler_params=pltpu.CompilerParams(vmem_limit_bytes=VMEM),
    )(*made)


def solution(mesh):
    in_specs = (
        P(),
        P("leaf", None),
        P("row", None),
        P("leaf", "row", "col"),
        P("leaf", "col", "row"),
        P("leaf", None, "row", "col"),
        P("leaf", "col", "row"),
        P("leaf", "row", "col"),
        P("leaf", "col", "row"),
    )
    out_specs = (
        P("leaf", "row", "col"),
        P("leaf", "col", "row"),
        P("leaf", None, "row", "col"),
        P("leaf", "col", "row"),
        P("leaf", None, "row", "col"),
        P("leaf", "col", "row"),
    )

    def whole(*args):
        return tuple(
            jax.shard_map(
                lambda *own: tuple(local(*own)),
                mesh=mesh,
                in_specs=in_specs,
                out_specs=out_specs,
                check_vma=False,
            )(*args)
        )

    return whole
```
